32 devices in a mesh: parts: 2 (over y), ctx: 4 (over z), head: 2 (over x), fsdp: 2 (over core).
Axes of the slice: x: 2, y: 2, z: 4, core: 2. Of those that a mesh axis runs over, the one named last changes fastest.
Arguments:
- mixer_input_channels: bfloat16 [4096, 4096], P(('parts', 'ctx'), ('head', 'fsdp')), parts along dimension 0, may hold values from -6 to 6
- gate_channels: bfloat16 [4096, 4096], P(('parts', 'ctx'), ('head', 'fsdp')), parts along dimension 0, may hold values from -6 to 6
- input_group_maps: bfloat16 [4096, 1024], P(('parts', 'ctx'), ('head', 'fsdp')), parts along dimension 0, may hold values from -6 to 6
- output_group_maps: bfloat16 [4096, 1024], P(('parts', 'ctx'), ('head', 'fsdp')), parts along dimension 0, may hold values from -6 to 6
- step_size_input: float32 [64, 4096], P(('head', 'fsdp'), ('parts', 'ctx')), parts along dimension 1, may hold values from -4 to 4
- resets: int32 [4096], P(('parts', 'ctx')), parts along dimension 0, may hold values 0 or 1
- head_decay_rate: float32 [64], P(('head', 'fsdp')), may hold values from 2e-07 to 0.035
- step_size_bias: float32 [64], P(('head', 'fsdp')), may hold values from -1 to 1
- skip: float32 [64], P(('head', 'fsdp')), may hold values from 0.5 to 1.5
- gated_norm_gain: float32 [4096], P(('head', 'fsdp')), may hold values from 0.5 to 1.5
- adapter_down_map: bfloat16 [4096, 64], P(('head', 'fsdp')), may hold values from -0.09375 to 0.09375
- adapter_up_map: bfloat16 [64, 4096], P(None, ('head', 'fsdp')), may hold values from -0.75 to 0.75
- frozen_mixed_gradient: bfloat16 [4096, 4096], P(('parts', 'ctx'), ('head', 'fsdp')), parts along dimension 0, may hold values from -6 to 6
- layer_output_gradient: bfloat16 [4096, 4096], P(('parts', 'ctx'), ('head', 'fsdp')), parts along dimension 0, may hold values from -6 to 6
Outputs:
- mixed: bfloat16 [4096, 4096], P(('parts', 'ctx'), ('head', 'fsdp')), parts along dimension 0
- adapter_output: bfloat16 [4096, 4096], P(('parts', 'ctx'), ('head', 'fsdp')), parts along dimension 0
- mixer_input_gradient: bfloat16 [4096, 4096], P(('parts', 'ctx'), ('head', 'fsdp')), parts along dimension 0
- gate_input_gradient: bfloat16 [4096, 4096], P(('parts', 'ctx'), ('head', 'fsdp')), parts along dimension 0
- input_maps_gradient: bfloat16 [4096, 1024], P(('parts', 'ctx'), ('head', 'fsdp')), parts along dimension 0
- output_maps_gradient: bfloat16 [4096, 1024], P(('parts', 'ctx'), ('head', 'fsdp')), parts along dimension 0
- step_size_gradient: float32 [64, 4096], P(('head', 'fsdp'), ('parts', 'ctx')), parts along dimension 1
- adapter_down_gradient: float32 [8192, 64], P(('parts', 'head', 'fsdp')), parts along dimension 0
- adapter_up_gradient: float32 [128, 4096], P('parts', ('head', 'fsdp')), parts along dimension 0
The draws below stay inside these ranges and needn't reach their ends.
There are 2 independent parts, one for each index of `parts`. The reference program is written for one: setup_inputs(seed, part) draws one part's arguments, and reference() takes and returns one part's arrays. A program takes and returns all parts, laid end to end along the dimension named above; an argument that names none is the same for every part. Nothing has to cross between parts.
All inputs are finite; a program needn't handle non-finite values. No bound on the sum of `resets` on one device may be relied on, other than what follows from the above.
Results may differ from the reference program's by a relative error of at most 0.0057.
Values sent between devices are 32-bit elements; how exact they have to be, the bound alone decides.
No kernel may reach another device: no remote copies, remote signals or barrier semaphores. Data moves between devices by JAX's collectives and lax.ppermute only.
A program may use at most 128 MiB of HBM per device.

```python
import math
from functools import partial
import jax
import jax.numpy as jnp
from jax import lax

MODEL_WIDTH = 4096
MIXER_HEADS = 64
HEAD_CHANNELS = 64
STATE = 128
GROUPS = 8
ADAPTER_RANK = 64
SPAN = 256
LENGTH = 2048


def draw_head_decay_rate(key, part):
    lower = math.log(4e-07)
    upper = math.log(0.035)
    return jnp.exp(jax.random.uniform(key, (MIXER_HEADS,), jnp.float32, lower, upper))


def plant(result, rng, smallest, largest):
    longest = result.shape.index(max(result.shape))
    spots = []
    for shift in (0, 1):
        where = [jax.random.randint(jax.random.fold_in(rng, axis), (), 0, length) for axis, length in enumerate(result.shape)]
        where[longest] = (where[longest] + shift) % result.shape[longest]
        spots.append(tuple(where))
    return result.at[spots[0]].set(smallest).at[spots[1]].set(largest)


def steps_of(rng, extent, shards, smallest, largest):
    def one(axis_at, parts):
        draws = jax.random.uniform(jax.random.fold_in(jax.random.fold_in(rng, 6), axis_at), (parts,), jnp.float32, smallest / len(shards), largest / len(shards))
        return jnp.repeat(jnp.exp(draws), extent[axis_at] // parts).reshape((-1,) + (1,) * (len(extent) - axis_at - 1))

    level = one(*shards[0])
    for cut in shards[1:]:
        level = level * one(*cut)
    return level


def bell_draw(own_key, dims, deviation, limit, split=(), kind=jnp.bfloat16):
    result = deviation * jax.random.normal(own_key, dims, jnp.float32)
    if split:
        result = result * steps_of(own_key, dims, split, -0.22, 0.18)
    return jnp.clip(result, -limit, limit).astype(kind)


def setup_inputs(seed: int = 0, part: int = 0) -> dict:
    streams_of = jax.random.split(jax.random.key(seed), 15)
    own_keys = jax.random.split(jax.random.fold_in(streams_of[14], part), 15)
    return {
        "mixer_input_channels": bell_draw(own_keys[0], (LENGTH, MIXER_HEADS * HEAD_CHANNELS), 1.0, 6.0, ((0, 4), (1, 4))),
        "gate_channels": bell_draw(own_keys[1], (LENGTH, MIXER_HEADS * HEAD_CHANNELS), 1.0, 6.0, ((0, 4), (1, 4))),
        "input_group_maps": bell_draw(own_keys[2], (LENGTH, GROUPS * STATE), 1.0, 6.0, ((0, 4), (1, 4))),
        "output_group_maps": bell_draw(own_keys[3], (LENGTH, GROUPS * STATE), 1.0, 6.0, ((0, 4), (1, 4))),
        "step_size_input": bell_draw(own_keys[4], (MIXER_HEADS, LENGTH), 1.0, 4.0, ((0, 4), (1, 4)), jnp.float32),
        "resets": plant((jax.random.randint(own_keys[5], (LENGTH,), 0, 4096) < 1).astype(jnp.int32), jax.random.fold_in(own_keys[5], 1), 0, 1),
        "head_decay_rate": draw_head_decay_rate(jax.random.fold_in(streams_of[14], 71), part),
        "step_size_bias": jnp.clip(jax.random.uniform(streams_of[7], (MIXER_HEADS,), jnp.float32, -1.0, 1.0) * steps_of(streams_of[7], (MIXER_HEADS,), ((0, 4),), -0.4, 0.0), -1.0, 1.0),
        "skip": jnp.clip(0.5 + 1.0 * jax.random.uniform(streams_of[8], (MIXER_HEADS,), jnp.float32) ** steps_of(streams_of[8], (MIXER_HEADS,), ((0, 4),), -0.2, 0.2), 0.5, 1.5),
        "gated_norm_gain": jnp.clip(1.0 + 0.1 * jax.random.normal(streams_of[9], (MIXER_HEADS * HEAD_CHANNELS,), jnp.float32), 0.5, 1.5),
        "adapter_down_map": bell_draw(streams_of[10], (MIXER_HEADS * HEAD_CHANNELS, ADAPTER_RANK), (MIXER_HEADS * HEAD_CHANNELS) ** -0.5, 0.09375, ((0, 4),)),
        "adapter_up_map": bell_draw(streams_of[11], (ADAPTER_RANK, MODEL_WIDTH), ADAPTER_RANK ** -0.5, 0.75, ((1, 4),)),
        "frozen_mixed_gradient": bell_draw(own_keys[12], (LENGTH, MIXER_HEADS * HEAD_CHANNELS), 1.0, 6.0, ((0, 4), (1, 4))),
        "layer_output_gradient": bell_draw(own_keys[13], (LENGTH, MODEL_WIDTH), 1.0, 6.0, ((0, 4), (1, 4))),
    }


eps = 1e-05
adapter_scale = 2.0
highest = lax.Precision.HIGHEST

def span_step(rates, state, pieces):
    x_part, b_part, c_part, dt_part, r_part = pieces
    width = r_part.shape[0]
    per_group = x_part.shape[1] // b_part.shape[1]
    cum_log = jnp.cumsum(-rates[:, None] * dt_part, axis=1)
    reset_ids = jnp.cumsum(r_part)
    places = jnp.arange(width)
    same_mask = (reset_ids[:, None] == reset_ids[None, :]) & (places[:, None] >= places[None, :])
    log_gap = cum_log[:, :, None] - cum_log[:, None, :]
    damping = jnp.where(same_mask[None], jnp.exp(jnp.where(same_mask[None], log_gap, 0.0)), 0.0)
    scores = jnp.repeat(jnp.einsum('rgn,sgn->grs', c_part, b_part, precision=highest), per_group, axis=0)
    b_heads = jnp.repeat(b_part, per_group, axis=1)
    c_heads = jnp.repeat(c_part, per_group, axis=1)
    weights = damping * scores * dt_part[:, None, :]
    y_loc = jnp.einsum('hrs,shp->rhp', weights, x_part, precision=highest)
    from_start = jnp.exp(cum_log) * (reset_ids == 0)[None, :]
    y_carry = jnp.einsum('rhn,hpn->rhp', c_heads, state, precision=highest) * from_start.T[:, :, None]
    to_end = jnp.exp(cum_log[:, -1:] - cum_log) * (reset_ids == reset_ids[-1])[None, :]
    total = jnp.exp(cum_log[:, -1]) * (reset_ids[-1] == 0)
    scaled = x_part * (to_end * dt_part).T[:, :, None]
    new_state = total[:, None, None] * state + jnp.einsum('shp,shn->hpn', scaled, b_heads, precision=highest)
    return (new_state, y_loc + y_carry)

def mixer(mixer_input_channels, gate_channels, input_group_maps, output_group_maps, step_size_input, resets, head_decay_rate, step_size_bias, skip, gated_norm_gain):
    seq_len, channels = mixer_input_channels.shape
    head_count = step_size_input.shape[0]
    head_dim = channels // head_count
    groups = input_group_maps.shape[1] // STATE
    per_group = head_count // groups
    spans = seq_len // SPAN
    inputs = mixer_input_channels.astype(jnp.float32).reshape(seq_len, head_count, head_dim)
    b_group = input_group_maps.astype(jnp.float32).reshape(spans, SPAN, groups, STATE)
    c_group = output_group_maps.astype(jnp.float32).reshape(spans, SPAN, groups, STATE)
    dt_full = jax.nn.softplus(step_size_input + step_size_bias[:, None])
    pieces = (inputs.reshape(spans, SPAN, head_count, head_dim), b_group, c_group, dt_full.reshape(head_count, spans, SPAN).transpose(1, 0, 2), resets.reshape(spans, SPAN))
    start = jnp.zeros((head_count, head_dim, STATE), jnp.float32)
    stepper = jax.checkpoint(partial(span_step, head_decay_rate))
    final, outputs = lax.scan(stepper, start, pieces)
    y_full = outputs.reshape(seq_len, head_count, head_dim) + skip[None, :, None] * inputs
    gates_in = gate_channels.astype(jnp.float32).reshape(seq_len, head_count, head_dim)
    gated = y_full * jax.nn.silu(gates_in)
    grouped = gated.reshape(seq_len, groups, per_group * head_dim)
    normed = grouped * lax.rsqrt(lax.optimization_barrier(jnp.mean(grouped * grouped, axis=-1, keepdims=True)) + eps)
    return normed.reshape(seq_len, channels) * gated_norm_gain[None, :]

def reference(mixer_input_channels, gate_channels, input_group_maps, output_group_maps, step_size_input, resets, head_decay_rate, step_size_bias, skip, gated_norm_gain, adapter_down_map, adapter_up_map, frozen_mixed_gradient, layer_output_gradient):

    def forward(x_arg, z_arg, b_arg, c_arg, dt_arg):
        return mixer(x_arg, z_arg, b_arg, c_arg, dt_arg, resets, head_decay_rate, step_size_bias, skip, gated_norm_gain)
    scaled_out, pullback = jax.vjp(forward, mixer_input_channels, gate_channels, input_group_maps, output_group_maps, step_size_input)
    mixed = scaled_out.astype(jnp.bfloat16)
    low_rank_projected = (adapter_scale * jnp.dot(mixed, adapter_down_map, preferred_element_type=jnp.float32)).astype(jnp.bfloat16)
    adapter_output = jnp.dot(low_rank_projected, adapter_up_map, preferred_element_type=jnp.float32).astype(jnp.bfloat16)
    low_rank_gradient = (adapter_scale * jnp.dot(layer_output_gradient, adapter_up_map.T, preferred_element_type=jnp.float32)).astype(jnp.bfloat16)
    mixed_gradient = frozen_mixed_gradient.astype(jnp.float32) + jnp.dot(low_rank_gradient, adapter_down_map.T, preferred_element_type=jnp.float32)
    mixer_input_gradient, gate_input_gradient, input_maps_gradient, output_maps_gradient, step_size_gradient = pullback(mixed_gradient)
    adapter_down_gradient = jnp.dot(mixed.T, low_rank_gradient, preferred_element_type=jnp.float32)
    adapter_up_gradient = jnp.dot(low_rank_projected.T, layer_output_gradient, preferred_element_type=jnp.float32)
    return (mixed, adapter_output, mixer_input_gradient.astype(jnp.bfloat16), gate_input_gradient.astype(jnp.bfloat16), input_maps_gradient.astype(jnp.bfloat16), output_maps_gradient.astype(jnp.bfloat16), step_size_gradient.astype(jnp.float32), adapter_down_gradient, adapter_up_gradient)
```

```python
import functools

import jax
import jax.numpy as jnp
from jax import lax
from jax.experimental import pallas as pl
from jax.experimental.pallas import tpu as pltpu
from jax.sharding import PartitionSpec as P

STATE = 128
HEAD = 64
ROWS = 32
EPS = 1e-05
SCALE = 2.0
VMEM = 32 * 2**20

f32 = jnp.float32
bf16 = jnp.bfloat16


def dot(left, right, left_dim, right_dim):
    return lax.dot_general(
        left, right, (((left_dim,), (right_dim,)), ((), ())), preferred_element_type=f32
    )


def split2(v):
    high = v.astype(bf16)
    return high, (v - high.astype(f32)).astype(bf16)


def split3(v):
    high = v.astype(bf16)
    rest = v - high.astype(f32)
    mid = rest.astype(bf16)
    return high, mid, (rest - mid.astype(f32)).astype(bf16)


def head_places(heads, channels):
    lane = lax.broadcasted_iota(jnp.int32, (heads, channels), 1)
    row = lax.broadcasted_iota(jnp.int32, (heads, channels), 0)
    return lane // HEAD == row


def spread(v, places):
    ones = places.astype(bf16)
    return dot(
        jnp.concatenate(split2(v), axis=0), jnp.concatenate([ones, ones], axis=0), 0, 0
    )


def head_column(row, heads, first):
    lane = lax.broadcasted_iota(jnp.int32, (heads, row.shape[1]), 1)
    place = lax.broadcasted_iota(jnp.int32, (heads, row.shape[1]), 0)
    return jnp.sum(jnp.where(lane == place + first, row, 0.0), axis=1, keepdims=True)


def spread_row(v, places):
    return jnp.sum(jnp.where(places, v, 0.0), axis=0, keepdims=True)


def running_sum(v, exclusive):
    rows, length = v.shape
    s = lax.broadcasted_iota(jnp.int32, (length, length), 0)
    r = lax.broadcasted_iota(jnp.int32, (length, length), 1)
    upper = ((s < r) if exclusive else (s <= r)).astype(bf16)
    sums = dot(jnp.concatenate(split3(v), axis=0), upper, 1, 0)
    return sums[:rows] + sums[rows : 2 * rows] + sums[2 * rows :]


def state_kernel(
    x, b, c, step, resets, rates, biases, xw, state, bend, cstart, small, rows, ids_row, ids_col, first
):
    heads, length = step.shape
    rate = head_column(rates[...], heads, first)
    bias = head_column(biases[...], heads, first)
    channels = x.shape[1]
    places = head_places(heads, channels)
    raw = step[...] + bias
    dt = jnp.maximum(raw, 0.0) + jnp.log1p(jnp.exp(-jnp.abs(raw)))
    log_step = -rate * dt
    s = lax.broadcasted_iota(jnp.int32, (length, length), 0)
    r = lax.broadcasted_iota(jnp.int32, (length, length), 1)
    upper = (s <= r).astype(bf16)
    lower = (s >= r).astype(bf16)
    marks = jnp.broadcast_to(resets[...].astype(f32), (8, length)).astype(bf16)
    sums = dot(jnp.concatenate((marks,) + split3(log_step), axis=0), upper, 1, 0)
    ids = sums[:8]
    cum = sums[8 : 8 + heads] + sums[8 + heads : 8 + 2 * heads] + sums[8 + 2 * heads :]
    id_cols = dot(lower, marks, 1, 1)
    ids_row[...] = ids
    ids_col[...] = id_cols
    last = cum[:, length - 1 :]
    last_id = ids[:1, length - 1 :]
    middle = 0.5 * last
    fall = jnp.exp(cum - middle)
    rise = jnp.exp(middle - cum)
    weight = dt * rise
    small[0:heads] = dt
    small[heads : 2 * heads] = fall
    small[2 * heads : 3 * heads] = rise
    small[3 * heads :] = raw
    half_row = spread_row(jnp.exp(middle), places)
    total = jnp.where(last_id == 0, half_row * half_row, 0.0)
    rows[0:1] = total
    rows[1:2] = half_row
    rows[2:8] = jnp.zeros((6, channels), f32)
    xw[...] = (x[...].astype(f32) * spread(weight, places)).astype(bf16)
    to_end = id_cols[:, :1] == last_id
    from_start = id_cols[:, :1] == 0
    bend[...] = jnp.where(to_end, b[...].astype(f32), 0.0).astype(bf16)
    cstart[...] = jnp.where(from_start, c[...].astype(f32), 0.0).astype(bf16)
    state[0:STATE] = dot(bend[...], xw[...], 0, 0) * half_row
    state[STATE:] = jnp.broadcast_to(total, (8, channels))


def score_kernel(b, c, ids_row, ids_col, xw, y_loc):
    length = b.shape[0]
    half = length // 2
    for i in range(2):
        here = pl.ds(i * half, half)
        total = None
        for j in range(i + 1):
            there = pl.ds(j * half, half)
            scores = dot(c[here], b[there], 1, 1)
            same = ids_col[here, 0:1] == ids_row[0:1, there]
            if i == j:
                r = lax.broadcasted_iota(jnp.int32, (half, half), 0)
                s = lax.broadcasted_iota(jnp.int32, (half, half), 1)
                same = same & (r >= s)
            m = jnp.where(same, scores, 0.0).astype(bf16)
            term = dot(m, xw[there], 1, 0)
            total = term if total is None else total + term
        y_loc[here] = total


def gather_incoming(near, far, mid):
    return near[0:STATE] + near[STATE : STATE + 1] * far[...] + mid[...]


def norm_kernel(*refs, first):
    refs = list(refs)
    (y_loc, cstart, near, far, mid, small, rows, x, gate, skips, gain, frozen) = refs[:12]
    (gu_here, gu_there, down) = refs[12:15]
    refs = refs[15:]
    u_before = None if first == 0 else refs.pop(0)
    (mixed, gate_grad, down_part, gye, scaled, state_grad, u_part, y_dot) = refs[:8]
    (inner, falls, g_mixed, product) = refs[8:]
    length, channels = x.shape
    heads = channels // HEAD
    skip = head_column(skips[...], heads, first)
    gu = (SCALE * (gu_here[...] + gu_there[...])).astype(bf16)
    places = head_places(heads, channels)
    scaled[...] = (gather_incoming(near, far, mid) * rows[1:2]).astype(bf16)
    inner[...] = y_loc[...] + dot(cstart[...], scaled[...], 1, 0)
    falls[...] = spread(small[heads : 2 * heads], places)
    g_mixed[...] = frozen[...].astype(f32) + dot(gu, down[...], 0, 0)
    skip_row = spread_row(skip, places)
    gain_row = gain[...]

    def tile(i, carry):
        at = pl.ds(pl.multiple_of(i * ROWS, ROWS), ROWS)
        fall = falls[at]
        within = inner[at]
        z = gate[at].astype(f32)
        y = fall * within + skip_row * x[at].astype(f32)
        sig = 0.5 * jnp.tanh(0.5 * z) + 0.5
        act = z * sig
        grouped = y * act
        inv = lax.rsqrt(jnp.sum(grouped * grouped, axis=1, keepdims=True) * (1.0 / channels) + EPS)
        normed = grouped * inv
        mixed[at] = (normed * gain_row).astype(bf16)
        g_norm = g_mixed[at] * gain_row
        mean = jnp.sum(g_norm * normed, axis=1, keepdims=True) * (1.0 / channels)
        g_grouped = inv * (g_norm - normed * mean)
        gate_grad[at] = (g_grouped * y * (sig + act * (1.0 - sig))).astype(bf16)
        g = (g_grouped * act * fall).astype(bf16)
        gye[at] = g
        high, low = split2(g.astype(f32) * within)
        product[0, at] = high
        product[1, at] = low
        return carry

    lax.fori_loop(0, length // ROWS, tile, 0, unroll=4)
    state_grad[0:STATE] = dot(cstart[...], gye[...], 0, 0) * rows[1:2]
    state_grad[STATE:] = jnp.broadcast_to(rows[0:1], (8, channels))
    u_here = dot(down[...], mixed[...], 1, 1)
    u_part[...] = u_here if first == 0 else u_here + u_before[...]
    down_part[...] = dot(gu, mixed[...], 1, 0)
    ones = places.astype(bf16)
    y_dot[...] = dot(ones, product[0], 1, 1) + dot(ones, product[1], 1, 1)


def pair_kernel(b, c, ids_row, ids_col, xw, gye, scaled_in, c_grad, z_loc, b_loc):
    length = b.shape[0]
    half = length // 2
    scaled = scaled_in[...]
    for i in range(2):
        here = pl.ds(i * half, half)
        carried = dot(gye[here], scaled, 1, 1)
        total = jnp.where(ids_col[here, 0:1] == 0, carried, 0.0)
        for j in range(i + 1):
            there = pl.ds(j * half, half)
            same = ids_col[here, 0:1] == ids_row[0:1, there]
            if i == j:
                r = lax.broadcasted_iota(jnp.int32, (half, half), 0)
                s = lax.broadcasted_iota(jnp.int32, (half, half), 1)
                same = same & (r >= s)
            pair = jnp.where(same, dot(gye[here], xw[there], 1, 1), 0.0).astype(bf16)
            total += dot(pair, b[there], 1, 0)
        c_grad[here] = total.astype(bf16)
    for j in range(2):
        there = pl.ds(j * half, half)
        z_total = None
        for i in range(j, 2):
            here = pl.ds(i * half, half)
            same = ids_col[there, 0:1] == ids_row[0:1, here]
            if i == j:
                s = lax.broadcasted_iota(jnp.int32, (half, half), 0)
                r = lax.broadcasted_iota(jnp.int32, (half, half), 1)
                same = same & (r >= s)
            m = jnp.where(same, dot(b[there], c[here], 1, 1), 0.0).astype(bf16)
            pair = jnp.where(same, dot(xw[there], gye[here], 1, 1), 0.0).astype(bf16)
            z_term = dot(m, gye[here], 1, 0)
            b_term = dot(pair, c[here], 1, 0)
            z_total = z_term if z_total is None else z_total + z_term
            b_total = b_term if i == j else b_total + b_term
        z_loc[there] = z_total
        b_loc[there] = b_total


def input_kernel(
    z_loc, b_loc, bend, ids_col, ids_row, xw, gye, near, far, mid, grad_dev, scaled_in, rows, small, skips,
    rates, y_dot,
    x_grad, b_grad, step_grad,
    inner, weights, rises, product,
    first,
):
    length, channels = xw.shape
    heads = channels // HEAD
    skip = head_column(skips[...], heads, first)
    rate = head_column(rates[...], heads, first)
    places = head_places(heads, channels)
    dt = small[0:heads]
    rise = small[2 * heads : 3 * heads]
    raw = small[3 * heads :]
    incoming = gather_incoming(near, far, mid)
    scaled = (incoming * rows[1:2]).astype(bf16)
    inner[...] = z_loc[...] + dot(bend[...], scaled, 1, 0)
    weights[...] = spread(dt * rise, places)
    rises[...] = spread(skip * rise, places)

    def tile(i, carry):
        at = pl.ds(pl.multiple_of(i * ROWS, ROWS), ROWS)
        z = inner[at]
        x_grad[at] = (weights[at] * z + rises[at] * gye[at].astype(f32)).astype(bf16)
        high, low = split2(xw[at].astype(f32) * z)
        product[0, at] = high
        product[1, at] = low
        return carry

    lax.fori_loop(0, length // ROWS, tile, 0, unroll=4)
    carried = dot(xw[...], scaled, 1, 1)
    to_end = ids_col[:, 0:1] == ids_row[0:1, length - 1 :]
    b_grad[...] = (b_loc[...] + jnp.where(to_end, carried, 0.0)).astype(bf16)
    ones = places.astype(bf16)
    x_dot = dot(ones, product[0], 1, 1) + dot(ones, product[1], 1, 1)
    crossing = jnp.sum(
        (rows[0:1] * incoming + grad_dev[0:STATE]) * scaled_in[...].astype(f32), axis=0, keepdims=True
    ) / rows[1:2]
    constant = jnp.sum(jnp.where(places, crossing, 0.0), axis=1, keepdims=True)
    g_log = running_sum(x_dot - y_dot[...], True) + constant
    g_dt = x_dot / dt - rate * g_log
    step_grad[...] = g_dt / (1.0 + jnp.exp(-raw))


def adapter_kernel(u_here, u_there, up, lo, out, up_part):
    u = (SCALE * (u_here[...] + u_there[...])).astype(bf16)
    out[...] = dot(u, up[...], 0, 0).astype(bf16)
    up_part[...] = dot(u, lo[...], 1, 0)


def rank_kernel(up, lo, part):
    part[...] = dot(up[...], lo[...], 1, 1)


def call(kernel, ins, outs, scratch=(), cost=1.0, name=None):
    in_specs, operands = [], []
    for array, block, index in ins:
        if block is None:
            block, index = array.shape, (0,) * array.ndim
        in_specs.append(pl.BlockSpec(block, functools.partial(lambda at, i: at, index)))
        operands.append(array)
    out_specs, out_shapes, aliases = [], [], {}
    for at, (shape, dtype, block, index, held) in enumerate(outs):
        if block is None:
            block, index = shape, (0,) * len(shape)
        out_specs.append(pl.BlockSpec(block, functools.partial(lambda at, i: at, index)))
        out_shapes.append(jax.ShapeDtypeStruct(shape, dtype))
        if held is not None:
            aliases[len(operands)] = at
            operands.append(held)
            in_specs.append(pl.BlockSpec(memory_space=pl.ANY))
    n_real = len(ins)
    n_held = len(operands) - n_real

    def body(*refs):
        kernel(*refs[:n_real], *refs[n_real + n_held :])

    return pl.pallas_call(
        body,
        grid=(1,),
        in_specs=in_specs,
        out_specs=out_specs,
        out_shape=out_shapes,
        scratch_shapes=list(scratch),
        input_output_aliases=aliases,
        compiler_params=pltpu.CompilerParams(vmem_limit_bytes=VMEM),
        cost_estimate=pl.CostEstimate(
            flops=0, bytes_accessed=int(cost * 3.69e6), transcendentals=0
        ),
        name=name,
    )(*operands)


def passed_on(part, axis, reverse):
    count = lax.axis_size(axis)
    state = part[:STATE]
    decay = part[STATE : STATE + 1]
    if count == 4:
        pairs = [(3, 2), (1, 0)] if reverse else [(0, 1), (2, 3)]
        source, far, mid = (2, 0, 1) if reverse else (1, 3, 2)
        near = lax.ppermute(part, axis, pairs)
        joined = decay * near[:STATE] + state
        return (
            near,
            lax.ppermute(joined, axis, [(source, far)]),
            lax.ppermute(joined, axis, [(source, mid)]),
        )
    incoming = jnp.zeros_like(state)
    out = state
    for hop in range(count - 1):
        pair = (count - 1 - hop, count - 2 - hop) if reverse else (hop, hop + 1)
        got = lax.ppermute(out, axis, [pair])
        incoming = incoming + got
        out = state + decay * got
    return jnp.concatenate([incoming, jnp.zeros_like(part[STATE:])]), incoming, jnp.zeros_like(state)


def exchange_pair(part, axes):
    other = None
    for axis in axes:
        count = lax.axis_size(axis)
        span = 1
        while span < count:
            part = part if other is None else part + other
            other = lax.ppermute(part, axis, [(i, i ^ span) for i in range(count)])
            span *= 2
    return part, other


def exchange_sum(part, axes):
    here, there = exchange_pair(part, axes)
    return here + there


def per_device(
    mixer_input_channels,
    gate_channels,
    input_group_maps,
    output_group_maps,
    step_size_input,
    resets,
    head_decay_rate,
    step_size_bias,
    skip,
    gated_norm_gain,
    adapter_down_map,
    adapter_up_map,
    frozen_mixed_gradient,
    layer_output_gradient,
):
    length, channels = mixer_input_channels.shape
    groups = input_group_maps.shape[1] // STATE
    heads = step_size_input.shape[0] // groups
    width = channels // groups
    rank = adapter_up_map.shape[0]
    resets = resets.reshape(1, length)
    rates = head_decay_rate.reshape(1, -1)
    biases = step_size_bias.reshape(1, -1)
    skips = skip.reshape(1, -1)
    down_map = adapter_down_map.T
    gains = gated_norm_gain.reshape(1, -1)

    def cols(array, g):
        return (array, (array.shape[0], array.shape[1] // groups), (0, g))

    def head_rows(array, g):
        return (array, (heads, array.shape[1]), (g, 0))

    def whole(array):
        return (array, None, None)

    def fresh(shape, dtype):
        return (shape, dtype, None, None, None)

    states = []
    for g in range(groups):
        states.append(
            call(
                functools.partial(state_kernel, first=g * heads),
                [
                    cols(mixer_input_channels, g),
                    cols(input_group_maps, g),
                    cols(output_group_maps, g),
                    head_rows(step_size_input, g),
                    whole(resets),
                    whole(rates),
                    whole(biases),
                ],
                [
                    fresh((length, width), bf16),
                    fresh((STATE + 8, width), f32),
                    fresh((length, STATE), bf16),
                    fresh((length, STATE), bf16),
                    fresh((4 * heads, length), f32),
                    fresh((8, width), f32),
                    fresh((8, length), f32),
                    fresh((length, 8), f32),
                ],
                cost=1.5,
                name="state",
            )
        )
    (gu_part,) = call(
        rank_kernel,
        [whole(adapter_up_map), whole(layer_output_gradient)],
        [fresh((rank, length), f32)],
        cost=1.0,
        name="rank",
    )
    gu = exchange_pair(gu_part, ("fsdp", "head"))
    y_locs = []
    for g in range(groups):
        xw, _, _, _, _, _, ids_row, ids_col = states[g]
        y_locs += call(
            score_kernel,
            [
                cols(input_group_maps, g),
                cols(output_group_maps, g),
                whole(ids_row),
                whole(ids_col),
                whole(xw),
            ],
            [fresh((length, width), f32)],
            cost=1.0,
            name="score",
        )
    entering = [passed_on(states[g][1], "ctx", False) for g in range(groups)]
    mixed = gate_grad = down_part = u_part = None
    normed = []
    for g in range(groups):
        xw, state, bend, cstart, small, rows, ids_row, ids_col = states[g]
        results = call(
            functools.partial(norm_kernel, first=g * heads),
            [
                whole(y_locs[g]),
                whole(cstart),
                *map(whole, entering[g]),
                whole(small),
                whole(rows),
                cols(mixer_input_channels, g),
                cols(gate_channels, g),
                whole(skips),
                cols(gains, g),
                cols(frozen_mixed_gradient, g),
                *map(whole, gu),
                cols(down_map, g),
            ]
            + ([] if g == 0 else [whole(u_part)]),
            [
                ((length, channels), bf16, (length, width), (0, g), mixed),
                ((length, channels), bf16, (length, width), (0, g), gate_grad),
                ((rank, channels), f32, (rank, width), (0, g), down_part),
                fresh((length, width), bf16),
                fresh((STATE, width), bf16),
                fresh((STATE + 8, width), f32),
                fresh((rank, length), f32),
                fresh((heads, length), f32),
            ],
            [
                pltpu.VMEM((length, width), f32),
                pltpu.VMEM((length, width), f32),
                pltpu.VMEM((length, width), f32),
                pltpu.VMEM((2, length, width), bf16),
            ],
            cost=4.0,
            name="norm",
        )
        mixed, gate_grad, down_part, gye, scaled, state_grad, u_part, y_dot = results
        normed.append((gye, scaled, state_grad, y_dot))
    leaving = [passed_on(normed[g][2], "ctx", True) for g in range(groups)]
    u = exchange_pair(u_part, ("fsdp", "head"))
    c_grad = None
    pairs = []
    for g in range(groups):
        xw, state, bend, cstart, small, rows, ids_row, ids_col = states[g]
        c_grad, z_loc, b_loc = call(
            pair_kernel,
            [
                cols(input_group_maps, g),
                cols(output_group_maps, g),
                whole(ids_row),
                whole(ids_col),
                whole(xw),
                whole(normed[g][0]),
                whole(normed[g][1]),
            ],
            [
                ((length, groups * STATE), bf16, (length, STATE), (0, g), c_grad),
                fresh((length, width), f32),
                fresh((length, STATE), f32),
            ],
            cost=2.0,
            name="pair",
        )
        pairs.append((z_loc, b_loc))
    down_sum = exchange_sum(down_part, ("ctx",))
    adapter_output, up_part = call(
        adapter_kernel,
        [*map(whole, u), whole(adapter_up_map), whole(layer_output_gradient)],
        [fresh((length, channels), bf16), fresh((rank, channels), f32)],
        cost=1.5,
        name="adapter",
    )
    up_sum = exchange_sum(up_part, ("ctx",))
    x_grad = b_grad = step_grad = None
    for g in range(groups):
        xw, state, bend, cstart, small, rows, ids_row, ids_col = states[g]
        x_grad, b_grad, step_grad = call(
            functools.partial(input_kernel, first=g * heads),
            [
                whole(pairs[g][0]),
                whole(pairs[g][1]),
                whole(bend),
                whole(ids_col),
                whole(ids_row),
                whole(xw),
                whole(normed[g][0]),
                *map(whole, leaving[g]),
                whole(normed[g][2]),
                whole(normed[g][1]),
                whole(rows),
                whole(small),
                whole(skips),
                whole(rates),
                whole(normed[g][3]),
            ],
            [
                ((length, channels), bf16, (length, width), (0, g), x_grad),
                ((length, groups * STATE), bf16, (length, STATE), (0, g), b_grad),
                ((groups * heads, length), f32, (heads, length), (g, 0), step_grad),
            ],
            [
                pltpu.VMEM((length, width), f32),
                pltpu.VMEM((length, width), f32),
                pltpu.VMEM((length, width), f32),
                pltpu.VMEM((2, length, width), bf16),
            ],
            cost=2.5,
            name="input",
        )
    return (
        mixed,
        adapter_output,
        x_grad,
        gate_grad,
        b_grad,
        c_grad,
        step_grad,
        down_sum.T,
        up_sum,
    )


def solution(mesh):
    rows_cols = P(("parts", "ctx"), ("head", "fsdp"))
    heads = P(("head", "fsdp"))
    in_specs = (
        rows_cols,
        rows_cols,
        rows_cols,
        rows_cols,
        P(("head", "fsdp"), ("parts", "ctx")),
        P(("parts", "ctx")),
        heads,
        heads,
        heads,
        heads,
        P(("head", "fsdp"), None),
        P(None, ("head", "fsdp")),
        rows_cols,
        rows_cols,
    )
    out_specs = (
        rows_cols,
        rows_cols,
        rows_cols,
        rows_cols,
        rows_cols,
        rows_cols,
        P(("head", "fsdp"), ("parts", "ctx")),
        P(("parts", "head", "fsdp"), None),
        P("parts", ("head", "fsdp")),
    )
    return jax.shard_map(
        per_device, mesh=mesh, in_specs=in_specs, out_specs=out_specs, check_vma=False
    )
```

```python
import functools

import jax
import jax.numpy as jnp
from jax import lax
from jax.experimental import pallas as pl
from jax.experimental.pallas import tpu as pltpu
from jax.sharding import PartitionSpec as P

STATE = 128
HEAD = 64
ROWS = 32
EPS = 1e-05
SCALE = 2.0
VMEM = 18 * 2**20
COST = 3.69e6

f32 = jnp.float32
bf16 = jnp.bfloat16


def dot(left, right, left_dim, right_dim):
    return lax.dot_general(
        left, right, (((left_dim,), (right_dim,)), ((), ())), preferred_element_type=f32
    )


def split2(v):
    high = v.astype(bf16)
    return high, (v - high.astype(f32)).astype(bf16)


def split3(v):
    high = v.astype(bf16)
    rest = v - high.astype(f32)
    mid = rest.astype(bf16)
    return high, mid, (rest - mid.astype(f32)).astype(bf16)


def head_places(heads, channels):
    lane = lax.broadcasted_iota(jnp.int32, (heads, channels), 1)
    row = lax.broadcasted_iota(jnp.int32, (heads, channels), 0)
    return lane // HEAD == row


def spread(v, places):
    ones = places.astype(bf16)
    return dot(
        jnp.concatenate(split2(v), axis=0), jnp.concatenate([ones, ones], axis=0), 0, 0
    )


def head_column(row, heads, first):
    lane = lax.broadcasted_iota(jnp.int32, (heads, row.shape[1]), 1)
    place = lax.broadcasted_iota(jnp.int32, (heads, row.shape[1]), 0)
    return jnp.sum(jnp.where(lane == place + first, row, 0.0), axis=1, keepdims=True)


def spread_row(v, places):
    return jnp.sum(jnp.where(places, v, 0.0), axis=0, keepdims=True)


def running_sum(v, exclusive):
    rows, length = v.shape
    s = lax.broadcasted_iota(jnp.int32, (length, length), 0)
    r = lax.broadcasted_iota(jnp.int32, (length, length), 1)
    upper = ((s < r) if exclusive else (s <= r)).astype(bf16)
    sums = dot(jnp.concatenate(split3(v), axis=0), upper, 1, 0)
    return sums[:rows] + sums[rows : 2 * rows] + sums[2 * rows :]


def state_kernel(
    x, b, c, step, resets, rates, biases, xw, state, bend, cstart, small, rows, ids_row, ids_col, first
):
    heads, length = step.shape
    rate = head_column(rates[...], heads, first)
    bias = head_column(biases[...], heads, first)
    channels = x.shape[1]
    places = head_places(heads, channels)
    raw = step[...] + bias
    dt = jnp.maximum(raw, 0.0) + jnp.log1p(jnp.exp(-jnp.abs(raw)))
    log_step = -rate * dt
    s = lax.broadcasted_iota(jnp.int32, (length, length), 0)
    r = lax.broadcasted_iota(jnp.int32, (length, length), 1)
    upper = (s <= r).astype(bf16)
    lower = (s >= r).astype(bf16)
    marks = jnp.broadcast_to(resets[...].astype(f32), (8, length)).astype(bf16)
    sums = dot(jnp.concatenate((marks,) + split3(log_step), axis=0), upper, 1, 0)
    ids = sums[:8]
    cum = sums[8 : 8 + heads] + sums[8 + heads : 8 + 2 * heads] + sums[8 + 2 * heads :]
    id_cols = dot(lower, marks, 1, 1)
    ids_row[...] = ids
    ids_col[...] = id_cols
    last = cum[:, length - 1 :]
    last_id = ids[:1, length - 1 :]
    middle = 0.5 * last
    fall = jnp.exp(cum - middle)
    rise = jnp.exp(middle - cum)
    weight = dt * rise
    small[0:heads] = dt
    small[heads : 2 * heads] = fall
    small[2 * heads : 3 * heads] = rise
    small[3 * heads :] = raw
    half_row = spread_row(jnp.exp(middle), places)
    total = jnp.where(last_id == 0, half_row * half_row, 0.0)
    rows[0:1] = total
    rows[1:2] = half_row
    rows[2:8] = jnp.zeros((6, channels), f32)
    xw[...] = (x[...].astype(f32) * spread(weight, places)).astype(bf16)
    to_end = id_cols[:, :1] == last_id
    from_start = id_cols[:, :1] == 0
    bend[...] = jnp.where(to_end, b[...].astype(f32), 0.0).astype(bf16)
    cstart[...] = jnp.where(from_start, c[...].astype(f32), 0.0).astype(bf16)
    state[...] = dot(bend[...], xw[...], 0, 0) * half_row


def score_kernel(b, c, ids_row, ids_col, xw, y_loc):
    length = b.shape[0]
    half = length // 2
    for i in range(2):
        here = pl.ds(i * half, half)
        total = None
        for j in range(i + 1):
            there = pl.ds(j * half, half)
            scores = dot(c[here], b[there], 1, 1)
            same = ids_col[here, 0:1] == ids_row[0:1, there]
            if i == j:
                r = lax.broadcasted_iota(jnp.int32, (half, half), 0)
                s = lax.broadcasted_iota(jnp.int32, (half, half), 1)
                same = same & (r >= s)
            m = jnp.where(same, scores, 0.0).astype(bf16)
            term = dot(m, xw[there], 1, 0)
            total = term if total is None else total + term
        y_loc[here] = total


def gather_incoming(near, far, mid):
    return near[...] + far[...] + mid[...]


def norm_kernel(*refs, first):
    refs = list(refs)
    (y_loc, cstart, near, far, mid, small, rows, x, gate, skips, gain, frozen) = refs[:12]
    (gu_here, gu_there, down) = refs[12:15]
    refs = refs[15:]
    u_before = None if first == 0 else refs.pop(0)
    (mixed, gate_grad, down_part, gye, scaled, state_grad, u_part, y_dot) = refs[:8]
    (inner, falls, g_mixed, product) = refs[8:]
    length, channels = x.shape
    heads = channels // HEAD
    skip = head_column(skips[...], heads, first)
    gu = (SCALE * (gu_here[...] + gu_there[...])).astype(bf16)
    places = head_places(heads, channels)
    scaled[...] = (gather_incoming(near, far, mid) * rows[1:2]).astype(bf16)
    inner[...] = y_loc[...] + dot(cstart[...], scaled[...], 1, 0)
    falls[...] = spread(small[heads : 2 * heads], places)
    g_mixed[...] = frozen[...].astype(f32) + dot(gu, down[...], 0, 0)
    skip_row = spread_row(skip, places)
    gain_row = gain[...]

    def tile(i, carry):
        at = pl.ds(pl.multiple_of(i * ROWS, ROWS), ROWS)
        fall = falls[at]
        within = inner[at]
        z = gate[at].astype(f32)
        y = fall * within + skip_row * x[at].astype(f32)
        sig = 0.5 * jnp.tanh(0.5 * z) + 0.5
        act = z * sig
        grouped = y * act
        inv = lax.rsqrt(jnp.sum(grouped * grouped, axis=1, keepdims=True) * (1.0 / channels) + EPS)
        normed = grouped * inv
        mixed[at] = (normed * gain_row).astype(bf16)
        g_norm = g_mixed[at] * gain_row
        mean = jnp.sum(g_norm * normed, axis=1, keepdims=True) * (1.0 / channels)
        g_grouped = inv * (g_norm - normed * mean)
        gate_grad[at] = (g_grouped * y * (sig + act * (1.0 - sig))).astype(bf16)
        g = (g_grouped * act * fall).astype(bf16)
        gye[at] = g
        high, low = split2(g.astype(f32) * within)
        product[0, at] = high
        product[1, at] = low
        return carry

    lax.fori_loop(0, length // ROWS, tile, 0, unroll=4)
    state_grad[...] = dot(cstart[...], gye[...], 0, 0) * rows[1:2]
    u_here = dot(down[...], mixed[...], 1, 1)
    u_part[...] = u_here if first == 0 else u_here + u_before[...]
    down_part[...] = dot(gu, mixed[...], 1, 0)
    ones = places.astype(bf16)
    y_dot[...] = dot(ones, product[0], 1, 1) + dot(ones, product[1], 1, 1)


def pair_kernel(b, c, ids_row, ids_col, xw, gye, scaled_in, c_grad, z_loc, b_loc):
    length = b.shape[0]
    half = length // 2
    scaled = scaled_in[...]
    for i in range(2):
        here = pl.ds(i * half, half)
        carried = dot(gye[here], scaled, 1, 1)
        total = jnp.where(ids_col[here, 0:1] == 0, carried, 0.0)
        for j in range(i + 1):
            there = pl.ds(j * half, half)
            same = ids_col[here, 0:1] == ids_row[0:1, there]
            if i == j:
                r = lax.broadcasted_iota(jnp.int32, (half, half), 0)
                s = lax.broadcasted_iota(jnp.int32, (half, half), 1)
                same = same & (r >= s)
            pair = jnp.where(same, dot(gye[here], xw[there], 1, 1), 0.0).astype(bf16)
            total += dot(pair, b[there], 1, 0)
        c_grad[here] = total.astype(bf16)
    for j in range(2):
        there = pl.ds(j * half, half)
        z_total = None
        for i in range(j, 2):
            here = pl.ds(i * half, half)
            same = ids_col[there, 0:1] == ids_row[0:1, here]
            if i == j:
                s = lax.broadcasted_iota(jnp.int32, (half, half), 0)
                r = lax.broadcasted_iota(jnp.int32, (half, half), 1)
                same = same & (r >= s)
            m = jnp.where(same, dot(b[there], c[here], 1, 1), 0.0).astype(bf16)
            pair = jnp.where(same, dot(xw[there], gye[here], 1, 1), 0.0).astype(bf16)
            z_term = dot(m, gye[here], 1, 0)
            b_term = dot(pair, c[here], 1, 0)
            z_total = z_term if z_total is None else z_total + z_term
            b_total = b_term if i == j else b_total + b_term
        z_loc[there] = z_total
        b_loc[there] = b_total


def input_kernel(
    z_loc, b_loc, bend, ids_col, ids_row, xw, gye, near, far, mid, grad_dev, scaled_in, rows, small, skips,
    rates, y_dot,
    x_grad, b_grad, step_grad,
    inner, weights, rises, product,
    first,
):
    length, channels = xw.shape
    heads = channels // HEAD
    skip = head_column(skips[...], heads, first)
    rate = head_column(rates[...], heads, first)
    places = head_places(heads, channels)
    dt = small[0:heads]
    rise = small[2 * heads : 3 * heads]
    raw = small[3 * heads :]
    incoming = gather_incoming(near, far, mid)
    scaled = (incoming * rows[1:2]).astype(bf16)
    inner[...] = z_loc[...] + dot(bend[...], scaled, 1, 0)
    weights[...] = spread(dt * rise, places)
    rises[...] = spread(skip * rise, places)

    def tile(i, carry):
        at = pl.ds(pl.multiple_of(i * ROWS, ROWS), ROWS)
        z = inner[at]
        x_grad[at] = (weights[at] * z + rises[at] * gye[at].astype(f32)).astype(bf16)
        high, low = split2(xw[at].astype(f32) * z)
        product[0, at] = high
        product[1, at] = low
        return carry

    lax.fori_loop(0, length // ROWS, tile, 0, unroll=4)
    carried = dot(xw[...], scaled, 1, 1)
    to_end = ids_col[:, 0:1] == ids_row[0:1, length - 1 :]
    b_grad[...] = (b_loc[...] + jnp.where(to_end, carried, 0.0)).astype(bf16)
    ones = places.astype(bf16)
    x_dot = dot(ones, product[0], 1, 1) + dot(ones, product[1], 1, 1)
    crossing = jnp.sum(
        (rows[0:1] * incoming + grad_dev[...]) * scaled_in[...].astype(f32), axis=0, keepdims=True
    ) / rows[1:2]
    constant = jnp.sum(jnp.where(places, crossing, 0.0), axis=1, keepdims=True)
    g_log = running_sum(x_dot - y_dot[...], True) + constant
    g_dt = x_dot / dt - rate * g_log
    step_grad[...] = g_dt / (1.0 + jnp.exp(-raw))


def adapter_kernel(u_here, u_there, up, lo, out, up_part):
    u = (SCALE * (u_here[...] + u_there[...])).astype(bf16)
    out[...] = dot(u, up[...], 0, 0).astype(bf16)
    up_part[...] = dot(u, lo[...], 1, 0)


def adapter_halves_kernel(odd, u_here, u_there, up, lo, down_part, out, up_keep, up_send, down_keep, down_send):
    u = (SCALE * (u_here[...] + u_there[...])).astype(bf16)
    out[...] = dot(u, up[...], 0, 0).astype(bf16)
    up_part = dot(u, lo[...], 1, 0)
    rows = up_keep.shape[0]
    is_odd = odd[0] == 1
    for keep, send, part in ((up_keep, up_send, up_part), (down_keep, down_send, down_part[...])):
        keep[...] = jnp.where(is_odd, part[rows:], part[:rows])
        send[...] = jnp.where(is_odd, part[:rows], part[rows:])


def join_kernel(odd, *refs):
    is_odd = odd[0] == 1
    for keep, other, out in (refs[0:2] + refs[4:5], refs[2:4] + refs[5:6]):
        rows = keep.shape[0]
        out[:rows] = jnp.where(is_odd, other[...], keep[...])
        out[rows:] = jnp.where(is_odd, keep[...], other[...])


def rank_kernel(up, lo, part):
    part[...] = dot(up[...], lo[...], 1, 1)


def call(kernel, ins, outs, scratch=(), cost=1.0, name=None):
    in_specs, operands = [], []
    for array, block, index in ins:
        if block == "scalar":
            in_specs.append(pl.BlockSpec(memory_space=pltpu.SMEM))
            operands.append(array)
            continue
        if block is None:
            block, index = array.shape, (0,) * array.ndim
        in_specs.append(pl.BlockSpec(block, functools.partial(lambda at, i: at, index)))
        operands.append(array)
    out_specs, out_shapes, aliases = [], [], {}
    for at, (shape, dtype, block, index, held) in enumerate(outs):
        if block is None:
            block, index = shape, (0,) * len(shape)
        out_specs.append(pl.BlockSpec(block, functools.partial(lambda at, i: at, index)))
        out_shapes.append(jax.ShapeDtypeStruct(shape, dtype))
        if held is not None:
            aliases[len(operands)] = at
            operands.append(held)
            in_specs.append(pl.BlockSpec(memory_space=pl.ANY))
    n_real = len(ins)
    n_held = len(operands) - n_real

    def body(*refs):
        kernel(*refs[:n_real], *refs[n_real + n_held :])

    return pl.pallas_call(
        body,
        grid=(1,),
        in_specs=in_specs,
        out_specs=out_specs,
        out_shape=out_shapes,
        scratch_shapes=list(scratch),
        input_output_aliases=aliases,
        compiler_params=pltpu.CompilerParams(vmem_limit_bytes=VMEM),
        cost_estimate=pl.CostEstimate(
            flops=0, bytes_accessed=int(cost * COST), transcendentals=0
        ),
        name=name,
    )(*operands)


def after(value, *others):
    return lax.optimization_barrier((value, *others))[0]


def hop(part, axis, *pairs):
    return lax.ppermute(part, axis, list(pairs))


def chain(state, decay, axis, reverse):
    count = lax.axis_size(axis)
    incoming = jnp.zeros_like(state)
    out = state
    for at in range(count - 1):
        got = hop(out, axis, (count - 1 - at, count - 2 - at) if reverse else (at, at + 1))
        incoming = incoming + got
        out = state + decay * got
    return incoming, jnp.zeros_like(state), jnp.zeros_like(state)


def exchange_pair(part, axes):
    other = None
    for axis in axes:
        count = lax.axis_size(axis)
        span = 1
        while span < count:
            part = part if other is None else part + other
            other = lax.ppermute(part, axis, [(i, i ^ span) for i in range(count)])
            span *= 2
    return part, other


def exchange_sum(part, axes):
    here, there = exchange_pair(part, axes)
    return here + there


def per_device(
    mixer_input_channels,
    gate_channels,
    input_group_maps,
    output_group_maps,
    step_size_input,
    resets,
    head_decay_rate,
    step_size_bias,
    skip,
    gated_norm_gain,
    adapter_down_map,
    adapter_up_map,
    frozen_mixed_gradient,
    layer_output_gradient,
):
    length, channels = mixer_input_channels.shape
    groups = input_group_maps.shape[1] // STATE
    heads = step_size_input.shape[0] // groups
    width = channels // groups
    rank = adapter_up_map.shape[0]
    resets = resets.reshape(1, length)
    rates = head_decay_rate.reshape(1, -1)
    biases = step_size_bias.reshape(1, -1)
    skips = skip.reshape(1, -1)
    down_map = adapter_down_map.T
    gains = gated_norm_gain.reshape(1, -1)

    def cols(array, g):
        return (array, (array.shape[0], array.shape[1] // groups), (0, g))

    def head_rows(array, g):
        return (array, (heads, array.shape[1]), (g, 0))

    def whole(array):
        return (array, None, None)

    def fresh(shape, dtype):
        return (shape, dtype, None, None, None)

    everything = range(groups)
    short = lax.axis_size("ctx") == 4

    def state_call(g, rates):
        return call(
            functools.partial(state_kernel, first=g * heads),
            [
                cols(mixer_input_channels, g),
                cols(input_group_maps, g),
                cols(output_group_maps, g),
                head_rows(step_size_input, g),
                whole(resets),
                whole(rates),
                whole(biases),
            ],
            [
                fresh((length, width), bf16),
                fresh((STATE, width), f32),
                fresh((length, STATE), bf16),
                fresh((length, STATE), bf16),
                fresh((4 * heads, length), f32),
                fresh((8, width), f32),
                fresh((8, length), f32),
                fresh((length, 8), f32),
            ],
            cost=1.5,
            name="state",
        )

    def score_call(g):
        xw, _, _, _, _, _, ids_row, ids_col = states[g]
        return call(
            score_kernel,
            [
                cols(input_group_maps, g),
                cols(output_group_maps, g),
                whole(ids_row),
                whole(ids_col),
                whole(xw),
            ],
            [fresh((length, width), f32)],
            cost=1.0,
            name="score",
        )[0]

    states, y_locs = [], []
    for g in everything:
        states.append(state_call(g, after(rates, y_locs[-1]) if g else rates))
        y_locs.append(score_call(g))
    (gu_part,) = call(
        rank_kernel,
        [whole(after(adapter_up_map, states[0][5])), whole(layer_output_gradient)],
        [fresh((rank, length), f32)],
        cost=1.0,
        name="rank",
    )
    gu = exchange_pair(gu_part, ("fsdp", "head"))
    parts = [states[g][1] for g in everything]
    decays = [states[g][5][0:1] for g in everything]
    entering = []
    if short:
        first = [hop(parts[0], "ctx", (0, 1))]
        for g in range(1, groups):
            first.append(hop(after(parts[g], first[-1]), "ctx", (0, 1)))
        for g in everything:
            joined = after(decays[g], parts[-1], gu[0]) * first[g] + parts[g]
            second = hop(joined, "ctx", (1, 2))
            joined = after(decays[g], y_locs[-1], gu[1]) * second + parts[g]
            entering.append((first[g], second, hop(joined, "ctx", (2, 3))))
    else:
        entering = [chain(parts[g], decays[g], "ctx", False) for g in everything]
    mixed = gate_grad = down_part = u_part = c_grad = None
    normed, pairs = [], []

    def pair_call(g, held, *others):
        xw, state, bend, cstart, small, rows, ids_row, ids_col = states[g]
        return call(
            pair_kernel,
            [
                cols(input_group_maps, g),
                cols(output_group_maps, g),
                whole(after(ids_row, *others) if others else ids_row),
                whole(ids_col),
                whole(xw),
                whole(normed[g][0]),
                whole(normed[g][1]),
            ],
            [
                ((length, groups * STATE), bf16, (length, STATE), (0, g), held),
                fresh((length, width), f32),
                fresh((length, STATE), f32),
            ],
            cost=2.0,
            name="pair",
        )

    for g in everything:
        xw, state, bend, cstart, small, rows, ids_row, ids_col = states[g]
        results = call(
            functools.partial(norm_kernel, first=g * heads),
            [
                whole(y_locs[g]),
                whole(cstart),
                *map(whole, entering[g]),
                whole(small),
                whole(rows),
                cols(mixer_input_channels, g),
                cols(gate_channels, g),
                whole(skips),
                cols(gains, g),
                cols(frozen_mixed_gradient, g),
                *map(whole, gu),
                cols(down_map, g),
            ]
            + ([] if g == 0 else [whole(u_part)]),
            [
                ((length, channels), bf16, (length, width), (0, g), mixed),
                ((length, channels), bf16, (length, width), (0, g), gate_grad),
                ((rank, channels), f32, (rank, width), (0, g), down_part),
                fresh((length, width), bf16),
                fresh((STATE, width), bf16),
                fresh((STATE, width), f32),
                fresh((rank, length), f32),
                fresh((heads, length), f32),
            ],
            [
                pltpu.VMEM((length, width), f32),
                pltpu.VMEM((length, width), f32),
                pltpu.VMEM((length, width), f32),
                pltpu.VMEM((2, length, width), bf16),
            ],
            cost=4.0,
            name="norm",
        )
        mixed, gate_grad, down_part, gye, scaled, state_grad, u_part, y_dot = results
        normed.append((gye, scaled, state_grad, y_dot))
    leaving = []
    if short:
        last = [hop(normed[g][2], "ctx", (3, 2)) for g in everything]
        joined = after(decays[0], u_part) * last[0] + normed[0][2]
        then = [hop(joined, "ctx", (2, 1))]
    u = exchange_pair(u_part, ("fsdp", "head"))
    half = fresh((rank // 2, channels), f32)
    if short:
        odd = (lax.axis_index("ctx") % 2).reshape(1)
        adapter_output, *halves = call(
            adapter_halves_kernel,
            [
                (odd, "scalar", None),
                *map(whole, u),
                whole(adapter_up_map),
                whole(layer_output_gradient),
                whole(down_part),
            ],
            [fresh((length, channels), bf16), half, half, half, half],
            cost=1.5,
            name="adapter",
        )
    else:
        adapter_output, up_part = call(
            adapter_kernel,
            [*map(whole, u), whole(adapter_up_map), whole(layer_output_gradient)],
            [fresh((length, channels), bf16), fresh((rank, channels), f32)],
            cost=1.5,
            name="adapter",
        )
    if short:
        for g in range(1, groups):
            joined = after(decays[g], halves[0]) * last[g] + normed[g][2]
            then.append(hop(joined, "ctx", (2, 1)))
    for g in everything:
        c_grad, z_loc, b_loc = pair_call(g, c_grad, *([joined] if short else []))
        pairs.append((z_loc, b_loc))
    if short:
        for g in everything:
            joined = after(decays[g], pairs[-1][1]) * then[g] + normed[g][2]
            leaving.append((last[g], then[g], hop(joined, "ctx", (1, 0))))
        neighbours = [(0, 1), (1, 0), (2, 3), (3, 2)]
        across = [(0, 2), (2, 0), (1, 3), (3, 1)]
        ends = []
        for keep, send in (halves[:2], halves[2:]):
            keep = keep + hop(send, "ctx", *neighbours)
            got = hop(keep, "ctx", *across)
            keep = after(keep, joined) + got
            ends += [keep, hop(keep, "ctx", *neighbours)]
        up_sum, down_sum = call(
            join_kernel,
            [(odd, "scalar", None), *map(whole, ends)],
            [fresh((rank, channels), f32), fresh((rank, channels), f32)],
            name="join",
        )
    else:
        up_sum = exchange_sum(up_part, ("ctx",))
        down_sum = exchange_sum(down_part, ("ctx",))
        leaving = [chain(normed[g][2], decays[g], "ctx", True) for g in everything]
    x_grad = b_grad = step_grad = None
    for g in everything:
        xw, state, bend, cstart, small, rows, ids_row, ids_col = states[g]
        x_grad, b_grad, step_grad = call(
            functools.partial(input_kernel, first=g * heads),
            [
                whole(pairs[g][0]),
                whole(pairs[g][1]),
                whole(bend),
                whole(ids_col),
                whole(ids_row),
                whole(xw),
                whole(normed[g][0]),
                *map(whole, leaving[g]),
                whole(normed[g][2]),
                whole(normed[g][1]),
                whole(rows),
                whole(small),
                whole(skips),
                whole(rates),
                whole(normed[g][3]),
            ],
            [
                ((length, channels), bf16, (length, width), (0, g), x_grad),
                ((length, groups * STATE), bf16, (length, STATE), (0, g), b_grad),
                ((groups * heads, length), f32, (heads, length), (g, 0), step_grad),
            ],
            [
                pltpu.VMEM((length, width), f32),
                pltpu.VMEM((length, width), f32),
                pltpu.VMEM((length, width), f32),
                pltpu.VMEM((2, length, width), bf16),
            ],
            cost=2.5,
            name="input",
        )
    return (
        mixed,
        adapter_output,
        x_grad,
        gate_grad,
        b_grad,
        c_grad,
        step_grad,
        down_sum.T,
        up_sum,
    )


def solution(mesh):
    rows_cols = P(("parts", "ctx"), ("head", "fsdp"))
    heads = P(("head", "fsdp"))
    in_specs = (
        rows_cols,
        rows_cols,
        rows_cols,
        rows_cols,
        P(("head", "fsdp"), ("parts", "ctx")),
        P(("parts", "ctx")),
        heads,
        heads,
        heads,
        heads,
        P(("head", "fsdp"), None),
        P(None, ("head", "fsdp")),
        rows_cols,
        rows_cols,
    )
    out_specs = (
        rows_cols,
        rows_cols,
        rows_cols,
        rows_cols,
        rows_cols,
        rows_cols,
        P(("head", "fsdp"), ("parts", "ctx")),
        P(("parts", "head", "fsdp"), None),
        P("parts", ("head", "fsdp")),
    )
    return jax.shard_map(
        per_device, mesh=mesh, in_specs=in_specs, out_specs=out_specs, check_vma=False
    )
```

```python
import functools

import jax
import jax.numpy as jnp
from jax import lax
from jax.experimental import pallas as pl
from jax.experimental.pallas import tpu as pltpu
from jax.sharding import PartitionSpec as P

STATE = 128
HEAD = 64
ROWS = 32
EPS = 1e-05
SCALE = 2.0
VMEM = 18 * 2**20
COST = 3.69e6

f32 = jnp.float32
bf16 = jnp.bfloat16


def dot(left, right, left_dim, right_dim):
    return lax.dot_general(
        left, right, (((left_dim,), (right_dim,)), ((), ())), preferred_element_type=f32
    )


def split2(v):
    high = v.astype(bf16)
    return high, (v - high.astype(f32)).astype(bf16)


def split3(v):
    high = v.astype(bf16)
    rest = v - high.astype(f32)
    mid = rest.astype(bf16)
    return high, mid, (rest - mid.astype(f32)).astype(bf16)


def head_places(heads, channels):
    lane = lax.broadcasted_iota(jnp.int32, (heads, channels), 1)
    row = lax.broadcasted_iota(jnp.int32, (heads, channels), 0)
    return lane // HEAD == row


def spread(v, places):
    ones = places.astype(bf16)
    return dot(
        jnp.concatenate(split2(v), axis=0), jnp.concatenate([ones, ones], axis=0), 0, 0
    )


def head_column(row, heads, first):
    lane = lax.broadcasted_iota(jnp.int32, (heads, row.shape[1]), 1)
    place = lax.broadcasted_iota(jnp.int32, (heads, row.shape[1]), 0)
    return jnp.sum(jnp.where(lane == place + first, row, 0.0), axis=1, keepdims=True)


def spread_row(v, places):
    return jnp.sum(jnp.where(places, v, 0.0), axis=0, keepdims=True)


def running_sum(v, exclusive):
    rows, length = v.shape
    s = lax.broadcasted_iota(jnp.int32, (length, length), 0)
    r = lax.broadcasted_iota(jnp.int32, (length, length), 1)
    upper = ((s < r) if exclusive else (s <= r)).astype(bf16)
    sums = dot(jnp.concatenate(split3(v), axis=0), upper, 1, 0)
    return sums[:rows] + sums[rows : 2 * rows] + sums[2 * rows :]


def state_kernel(
    x, b, c, step, resets, rates, biases, xw, state, bend, cstart, small, rows, ids_row, ids_col, first
):
    heads, length = step.shape
    rate = head_column(rates[...], heads, first)
    bias = head_column(biases[...], heads, first)
    channels = x.shape[1]
    places = head_places(heads, channels)
    raw = step[...] + bias
    dt = jnp.maximum(raw, 0.0) + jnp.log1p(jnp.exp(-jnp.abs(raw)))
    log_step = -rate * dt
    s = lax.broadcasted_iota(jnp.int32, (length, length), 0)
    r = lax.broadcasted_iota(jnp.int32, (length, length), 1)
    upper = (s <= r).astype(bf16)
    lower = (s >= r).astype(bf16)
    marks = jnp.broadcast_to(resets[...].astype(f32), (8, length)).astype(bf16)
    sums = dot(jnp.concatenate((marks,) + split3(log_step), axis=0), upper, 1, 0)
    ids = sums[:8]
    cum = sums[8 : 8 + heads] + sums[8 + heads : 8 + 2 * heads] + sums[8 + 2 * heads :]
    id_cols = dot(lower, marks, 1, 1)
    ids_row[...] = ids
    ids_col[...] = id_cols
    last = cum[:, length - 1 :]
    last_id = ids[:1, length - 1 :]
    middle = 0.5 * last
    fall = jnp.exp(cum - middle)
    rise = jnp.exp(middle - cum)
    weight = dt * rise
    small[0:heads] = dt
    small[heads : 2 * heads] = fall
    small[2 * heads : 3 * heads] = rise
    small[3 * heads :] = raw
    half_row = spread_row(jnp.exp(middle), places)
    total = jnp.where(last_id == 0, half_row * half_row, 0.0)
    rows[0:1] = total
    rows[1:2] = half_row
    rows[2:8] = jnp.zeros((6, channels), f32)
    xw[...] = (x[...].astype(f32) * spread(weight, places)).astype(bf16)
    to_end = id_cols[:, :1] == last_id
    from_start = id_cols[:, :1] == 0
    bend[...] = jnp.where(to_end, b[...].astype(f32), 0.0).astype(bf16)
    cstart[...] = jnp.where(from_start, c[...].astype(f32), 0.0).astype(bf16)
    state[...] = dot(bend[...], xw[...], 0, 0) * half_row


def score_kernel(b, c, ids_row, ids_col, xw, y_loc):
    length = b.shape[0]
    half = length // 2
    for i in range(2):
        here = pl.ds(i * half, half)
        total = None
        for j in range(i + 1):
            there = pl.ds(j * half, half)
            scores = dot(c[here], b[there], 1, 1)
            same = ids_col[here, 0:1] == ids_row[0:1, there]
            if i == j:
                r = lax.broadcasted_iota(jnp.int32, (half, half), 0)
                s = lax.broadcasted_iota(jnp.int32, (half, half), 1)
                same = same & (r >= s)
            m = jnp.where(same, scores, 0.0).astype(bf16)
            term = dot(m, xw[there], 1, 0)
            total = term if total is None else total + term
        y_loc[here] = total


def gather_incoming(near, far, mid):
    return near[...] + far[...] + mid[...]


def norm_kernel(*refs, first):
    refs = list(refs)
    (y_loc, cstart, near, far, mid, small, rows, x, gate, skips, gain, frozen) = refs[:12]
    (gu_here, gu_there, down) = refs[12:15]
    refs = refs[15:]
    u_before = None if first == 0 else refs.pop(0)
    (mixed, gate_grad, down_part, gye, scaled, state_grad, u_part, y_dot) = refs[:8]
    (inner, falls, g_mixed, product) = refs[8:]
    length, channels = x.shape
    heads = channels // HEAD
    skip = head_column(skips[...], heads, first)
    gu = (SCALE * (gu_here[...] + gu_there[...])).astype(bf16)
    places = head_places(heads, channels)
    scaled[...] = (gather_incoming(near, far, mid) * rows[1:2]).astype(bf16)
    inner[...] = y_loc[...] + dot(cstart[...], scaled[...], 1, 0)
    falls[...] = spread(small[heads : 2 * heads], places)
    g_mixed[...] = dot(gu, down[...], 0, 0)
    skip_row = spread_row(skip, places)
    gain_row = gain[...]

    def tile(i, carry):
        at = pl.ds(pl.multiple_of(i * ROWS, ROWS), ROWS)
        fall = falls[at]
        within = inner[at]
        z = gate[at].astype(f32)
        y = fall * within + skip_row * x[at].astype(f32)
        sig = 0.5 * jnp.tanh(0.5 * z) + 0.5
        act = z * sig
        grouped = y * act
        inv = lax.rsqrt(jnp.sum(grouped * grouped, axis=1, keepdims=True) * (1.0 / channels) + EPS)
        normed = grouped * inv
        mixed[at] = (normed * gain_row).astype(bf16)
        g_norm = (frozen[at].astype(f32) + g_mixed[at]) * gain_row
        mean = jnp.sum(g_norm * normed, axis=1, keepdims=True) * (1.0 / channels)
        g_grouped = inv * (g_norm - normed * mean)
        gate_grad[at] = (g_grouped * y * (sig + act * (1.0 - sig))).astype(bf16)
        g = (g_grouped * act * fall).astype(bf16)
        gye[at] = g
        high, low = split2(g.astype(f32) * within)
        product[0, at] = high
        product[1, at] = low
        return carry

    lax.fori_loop(0, length // ROWS, tile, 0, unroll=4)
    state_grad[...] = dot(cstart[...], gye[...], 0, 0) * rows[1:2]
    u_here = dot(down[...], mixed[...], 1, 1)
    u_part[...] = u_here if first == 0 else u_here + u_before[...]
    down_part[...] = dot(gu, mixed[...], 1, 0)
    ones = places.astype(bf16)
    y_dot[...] = dot(ones, product[0], 1, 1) + dot(ones, product[1], 1, 1)


def pair_kernel(b, c, ids_row, ids_col, xw, gye, scaled_in, c_grad, z_loc, b_loc):
    length = b.shape[0]
    half = length // 2
    scaled = scaled_in[...]
    for i in range(2):
        here = pl.ds(i * half, half)
        carried = dot(gye[here], scaled, 1, 1)
        total = jnp.where(ids_col[here, 0:1] == 0, carried, 0.0)
        for j in range(i + 1):
            there = pl.ds(j * half, half)
            same = ids_col[here, 0:1] == ids_row[0:1, there]
            if i == j:
                r = lax.broadcasted_iota(jnp.int32, (half, half), 0)
                s = lax.broadcasted_iota(jnp.int32, (half, half), 1)
                same = same & (r >= s)
            pair = jnp.where(same, dot(gye[here], xw[there], 1, 1), 0.0).astype(bf16)
            total += dot(pair, b[there], 1, 0)
        c_grad[here] = total.astype(bf16)
    for j in range(2):
        there = pl.ds(j * half, half)
        z_total = None
        for i in range(j, 2):
            here = pl.ds(i * half, half)
            same = ids_col[there, 0:1] == ids_row[0:1, here]
            if i == j:
                s = lax.broadcasted_iota(jnp.int32, (half, half), 0)
                r = lax.broadcasted_iota(jnp.int32, (half, half), 1)
                same = same & (r >= s)
            m = jnp.where(same, dot(b[there], c[here], 1, 1), 0.0).astype(bf16)
            pair = jnp.where(same, dot(xw[there], gye[here], 1, 1), 0.0).astype(bf16)
            z_term = dot(m, gye[here], 1, 0)
            b_term = dot(pair, c[here], 1, 0)
            z_total = z_term if z_total is None else z_total + z_term
            b_total = b_term if i == j else b_total + b_term
        z_loc[there] = z_total
        b_loc[there] = b_total


def input_kernel(
    z_loc, b_loc, bend, ids_col, ids_row, xw, gye, near, far, mid, grad_dev, scaled_in, rows, small, skips,
    rates, y_dot, passing,
    x_grad, b_grad, step_grad, passed,
    inner, weights, rises, product,
    first,
):
    length, channels = xw.shape
    heads = channels // HEAD
    skip = head_column(skips[...], heads, first)
    rate = head_column(rates[...], heads, first)
    places = head_places(heads, channels)
    dt = small[0:heads]
    rise = small[2 * heads : 3 * heads]
    raw = small[3 * heads :]
    incoming = gather_incoming(near, far, mid)
    passed[...] = passing[...]
    scaled = (incoming * rows[1:2]).astype(bf16)
    inner[...] = z_loc[...] + dot(bend[...], scaled, 1, 0)
    weights[...] = spread(dt * rise, places)
    rises[...] = spread(skip * rise, places)

    def tile(i, carry):
        at = pl.ds(pl.multiple_of(i * ROWS, ROWS), ROWS)
        z = inner[at]
        x_grad[at] = (weights[at] * z + rises[at] * gye[at].astype(f32)).astype(bf16)
        high, low = split2(xw[at].astype(f32) * z)
        product[0, at] = high
        product[1, at] = low
        return carry

    lax.fori_loop(0, length // ROWS, tile, 0, unroll=4)
    carried = dot(xw[...], scaled, 1, 1)
    to_end = ids_col[:, 0:1] == ids_row[0:1, length - 1 :]
    b_grad[...] = (b_loc[...] + jnp.where(to_end, carried, 0.0)).astype(bf16)
    ones = places.astype(bf16)
    x_dot = dot(ones, product[0], 1, 1) + dot(ones, product[1], 1, 1)
    crossing = jnp.sum(
        (rows[0:1] * incoming + grad_dev[...]) * scaled_in[...].astype(f32), axis=0, keepdims=True
    ) / rows[1:2]
    constant = jnp.sum(jnp.where(places, crossing, 0.0), axis=1, keepdims=True)
    g_log = running_sum(x_dot - y_dot[...], True) + constant
    g_dt = x_dot / dt - rate * g_log
    step_grad[...] = g_dt / (1.0 + jnp.exp(-raw))


def adapter_kernel(u_here, u_there, up, lo, out, up_part):
    u = (SCALE * (u_here[...] + u_there[...])).astype(bf16)
    out[...] = dot(u, up[...], 0, 0).astype(bf16)
    up_part[...] = dot(u, lo[...], 1, 0)


def output_kernel(u, up, out):
    out[...] = dot(u[...], up[...], 0, 0).astype(bf16)


def halves_kernel(odd, u_here, u_there, lo, down_part, u_out, keep, send):
    u = (SCALE * (u_here[...] + u_there[...])).astype(bf16)
    u_out[...] = u
    rows = keep.shape[0] // 2
    is_odd = odd[0] == 1
    down = down_part[...]
    keep[rows:] = jnp.where(is_odd, down[rows:], down[:rows])
    send[rows:] = jnp.where(is_odd, down[:rows], down[rows:])
    up_part = dot(u, lo[...], 1, 0)
    keep[:rows] = jnp.where(is_odd, up_part[rows:], up_part[:rows])
    send[:rows] = jnp.where(is_odd, up_part[:rows], up_part[rows:])


def join_kernel(odd, keep, other, up_out, down_out):
    is_odd = odd[0] == 1
    rows = keep.shape[0] // 2
    for at, out in ((pl.ds(0, rows), up_out), (pl.ds(rows, rows), down_out)):
        out[:rows] = jnp.where(is_odd, other[at], keep[at])
        out[rows:] = jnp.where(is_odd, keep[at], other[at])


def rank_kernel(up, lo, part):
    part[...] = dot(up[...], lo[...], 1, 1)


def call(kernel, ins, outs, scratch=(), cost=1.0, name=None):
    in_specs, operands = [], []
    for array, block, index, *pinned in ins:
        if pinned:
            array = pltpu.with_memory_space_constraint(array, pltpu.HBM)
        if block in ("scalar", "far"):
            space = pltpu.SMEM if block == "scalar" else pltpu.HBM
            in_specs.append(pl.BlockSpec(memory_space=space))
            operands.append(array)
            continue
        if block is None:
            block, index = array.shape, (0,) * array.ndim
        in_specs.append(pl.BlockSpec(block, functools.partial(lambda at, i: at, index)))
        operands.append(array)
    out_specs, out_shapes, aliases = [], [], {}
    for at, (shape, dtype, block, index, held, *pinned) in enumerate(outs):
        if block is None:
            block, index = shape, (0,) * len(shape)
        out_specs.append(pl.BlockSpec(block, functools.partial(lambda at, i: at, index)))
        out_shapes.append((pltpu.HBM if pinned else jax.ShapeDtypeStruct)(shape, dtype))
        if held is not None:
            aliases[len(operands)] = at
            operands.append(held)
            in_specs.append(pl.BlockSpec(memory_space=pl.ANY))
    n_real = len(ins)
    n_held = len(operands) - n_real

    def body(*refs):
        kernel(*refs[:n_real], *refs[n_real + n_held :])

    return pl.pallas_call(
        body,
        grid=(1,),
        in_specs=in_specs,
        out_specs=out_specs,
        out_shape=out_shapes,
        scratch_shapes=list(scratch),
        input_output_aliases=aliases,
        compiler_params=pltpu.CompilerParams(vmem_limit_bytes=VMEM),
        cost_estimate=pl.CostEstimate(
            flops=0, bytes_accessed=int(cost * COST), transcendentals=0
        ),
        name=name,
    )(*operands)


def after(value, *others):
    return lax.optimization_barrier((value, *others))[0]


def hop(part, axis, *pairs):
    return lax.ppermute(part, axis, list(pairs))


def chain(state, decay, axis, reverse):
    count = lax.axis_size(axis)
    incoming = jnp.zeros_like(state)
    out = state
    for at in range(count - 1):
        got = hop(out, axis, (count - 1 - at, count - 2 - at) if reverse else (at, at + 1))
        incoming = incoming + got
        out = state + decay * got
    return incoming, jnp.zeros_like(state), jnp.zeros_like(state)


def exchange_pair(part, axes, *before):
    other = None
    for axis in axes:
        count = lax.axis_size(axis)
        span = 1
        while span < count:
            part = part if other is None else after(part, *before) + other
            other = lax.ppermute(part, axis, [(i, i ^ span) for i in range(count)])
            span *= 2
    return part, other


def exchange_sum(part, axes):
    here, there = exchange_pair(part, axes)
    return here + there


def per_device(
    mixer_input_channels,
    gate_channels,
    input_group_maps,
    output_group_maps,
    step_size_input,
    resets,
    head_decay_rate,
    step_size_bias,
    skip,
    gated_norm_gain,
    adapter_down_map,
    adapter_up_map,
    frozen_mixed_gradient,
    layer_output_gradient,
):
    length, channels = mixer_input_channels.shape
    groups = input_group_maps.shape[1] // STATE
    heads = step_size_input.shape[0] // groups
    width = channels // groups
    rank = adapter_up_map.shape[0]
    resets = resets.reshape(1, length)
    rates = head_decay_rate.reshape(1, -1)
    biases = step_size_bias.reshape(1, -1)
    skips = skip.reshape(1, -1)
    down_map = adapter_down_map.T
    gains = gated_norm_gain.reshape(1, -1)

    def cols(array, g):
        return (array, (array.shape[0], array.shape[1] // groups), (0, g))

    def head_rows(array, g):
        return (array, (heads, array.shape[1]), (g, 0))

    def whole(array):
        return (array, None, None)

    def fresh(shape, dtype):
        return (shape, dtype, None, None, None)

    def far(array):
        return (array, "far", None, True)

    def slow(item):
        return (*item, True)

    everything = range(groups)
    short = lax.axis_size("ctx") == 4

    def state_call(g, rates):
        return call(
            functools.partial(state_kernel, first=g * heads),
            [
                slow(cols(mixer_input_channels, g)),
                slow(cols(input_group_maps, g)),
                slow(cols(output_group_maps, g)),
                slow(head_rows(step_size_input, g)),
                slow(whole(resets)),
                slow(whole(rates)),
                slow(whole(biases)),
            ],
            [
                fresh((length, width), bf16),
                fresh((STATE, width), f32),
                fresh((length, STATE), bf16),
                fresh((length, STATE), bf16),
                fresh((4 * heads, length), f32),
                fresh((8, width), f32),
                fresh((8, length), f32),
                fresh((length, 8), f32),
            ],
            cost=1.5,
            name="state",
        )

    def score_call(g):
        xw, _, _, _, _, _, ids_row, ids_col = states[g]
        return call(
            score_kernel,
            [
                cols(input_group_maps, g),
                cols(output_group_maps, g),
                whole(ids_row),
                whole(ids_col),
                whole(xw),
            ],
            [fresh((length, width), f32)],
            cost=1.0,
            name="score",
        )[0]

    states, y_locs = [], []
    for g in everything:
        states.append(state_call(g, after(rates, y_locs[-1]) if g else rates))
        y_locs.append(score_call(g))
    (gu_part,) = call(
        rank_kernel,
        [whole(after(adapter_up_map, states[0][5])), whole(layer_output_gradient)],
        [fresh((rank, length), f32)],
        cost=1.0,
        name="rank",
    )
    parts = [states[g][1] for g in everything]
    decays = [states[g][5][0:1] for g in everything]
    entering = []
    if short:
        first = [hop(parts[g], "ctx", (0, 1)) for g in everything]
        joined = [after(decays[g], parts[-1], gu_part) * first[g] + parts[g] for g in everything]
        gu = exchange_pair(gu_part, ("fsdp", "head"), joined[0])
        for g in everything:
            second = hop(joined[g], "ctx", (1, 2))
            third = after(decays[g], y_locs[-1], gu[1]) * second + parts[g]
            entering.append((first[g], second, hop(third, "ctx", (2, 3))))
    else:
        gu = exchange_pair(gu_part, ("fsdp", "head"))
        entering = [chain(parts[g], decays[g], "ctx", False) for g in everything]
    mixed = gate_grad = down_part = u_part = c_grad = None
    normed, pairs = [], []

    def pair_call(g, held, *others):
        xw, state, bend, cstart, small, rows, ids_row, ids_col = states[g]
        return call(
            pair_kernel,
            [
                cols(input_group_maps, g),
                cols(output_group_maps, g),
                whole(after(ids_row, *others) if others else ids_row),
                whole(ids_col),
                whole(xw),
                whole(normed[g][0]),
                whole(normed[g][1]),
            ],
            [
                ((length, groups * STATE), bf16, (length, STATE), (0, g), held),
                fresh((length, width), f32),
                fresh((length, STATE), f32),
            ],
            cost=2.0,
            name="pair",
        )

    for g in everything:
        xw, state, bend, cstart, small, rows, ids_row, ids_col = states[g]
        results = call(
            functools.partial(norm_kernel, first=g * heads),
            [
                whole(y_locs[g]),
                whole(cstart),
                *map(whole, entering[g]),
                whole(small),
                whole(rows),
                cols(mixer_input_channels, g),
                cols(gate_channels, g),
                whole(skips),
                cols(gains, g),
                cols(frozen_mixed_gradient, g),
                *map(whole, gu),
                cols(down_map, g),
            ]
            + ([] if g == 0 else [whole(u_part)]),
            [
                ((length, channels), bf16, (length, width), (0, g), mixed),
                ((length, channels), bf16, (length, width), (0, g), gate_grad),
                slow(((rank, channels), f32, (rank, width), (0, g), down_part)),
                fresh((length, width), bf16),
                fresh((STATE, width), bf16),
                fresh((STATE, width), f32),
                fresh((rank, length), f32),
                slow(fresh((heads, length), f32)),
            ],
            [
                pltpu.VMEM((length, width), f32),
                pltpu.VMEM((length, width), f32),
                pltpu.VMEM((length, width), f32),
                pltpu.VMEM((2, length, width), bf16),
            ],
            cost=4.0,
            name="norm",
        )
        mixed, gate_grad, down_part, gye, scaled, state_grad, u_part, y_dot = results
        normed.append((gye, scaled, state_grad, y_dot))
    def input_call(g, leaving, held, passing, *before):
        xw, state, bend, cstart, small, rows, ids_row, ids_col = states[g]
        x_grad, b_grad, step_grad = held
        return call(
            functools.partial(input_kernel, first=g * heads),
            [
                whole(pairs[g][0]),
                whole(pairs[g][1]),
                whole(bend),
                whole(ids_col),
                whole(ids_row),
                whole(xw),
                whole(normed[g][0]),
                *map(whole, leaving),
                whole(normed[g][2]),
                whole(normed[g][1]),
                whole(rows),
                whole(small),
                whole(skips),
                whole(after(rates, *before) if before else rates),
                slow(whole(normed[g][3])),
                whole(passing),
            ],
            [
                ((length, channels), bf16, (length, width), (0, g), x_grad),
                ((length, groups * STATE), bf16, (length, STATE), (0, g), b_grad),
                ((groups * heads, length), f32, (heads, length), (g, 0), step_grad),
                fresh(passing.shape, f32),
            ],
            [
                pltpu.VMEM((length, width), f32),
                pltpu.VMEM((length, width), f32),
                pltpu.VMEM((length, width), f32),
                pltpu.VMEM((2, length, width), bf16),
            ],
            cost=2.5,
            name="input",
        )

    state_grads = [normed[g][2] for g in everything]
    held = (None, None, None)
    if short and groups == 2:
        neighbours = [(0, 1), (1, 0), (2, 3), (3, 2)]
        across = [(0, 2), (2, 0), (1, 3), (3, 1)]
        last = [hop(state_grads[g], "ctx", (3, 2)) for g in everything]
        sent = after(decays[0], u_part) * last[0] + state_grads[0]
        then = [hop(sent, "ctx", (2, 1))]
        u = exchange_pair(u_part, ("fsdp", "head"), sent)
        odd = (lax.axis_index("ctx") % 2).reshape(1)
        half = fresh((rank, channels), f32)
        u, keep, send = call(
            halves_kernel,
            [
                (odd, "scalar", None),
                *map(whole, u),
                whole(layer_output_gradient),
                slow(whole(down_part)),
            ],
            [fresh((rank, length), bf16), half, half],
            cost=1.5,
            name="halves",
        )
        sent = after(decays[1], keep) * last[1] + state_grads[1]
        then.append(hop(sent, "ctx", (2, 1)))
        got = hop(send, "ctx", *neighbours)
        sent = after(decays[0], sent) * then[0] + state_grads[0]
        ahead = [hop(sent, "ctx", (1, 0))]
        c_grad, *pair = pair_call(0, c_grad, sent)
        pairs.append(pair)
        keep = after(keep, pair[1]) + got
        got = hop(keep, "ctx", *across)
        *held, decay = input_call(0, (last[0], then[0], ahead[0]), held, decays[1], keep)
        sent = decay * then[1] + state_grads[1]
        ahead.append(hop(sent, "ctx", (1, 0)))
        c_grad, *pair = pair_call(1, c_grad, sent)
        pairs.append(pair)
        (adapter_output,) = call(
            output_kernel,
            [whole(after(u, sent)), whole(adapter_up_map)],
            [fresh((length, channels), bf16)],
            name="output",
        )
        keep = after(keep, sent, pair[1]) + got
        got = hop(keep, "ctx", *neighbours)
        *held, _ = input_call(1, (last[1], then[1], ahead[1]), held, decays[1])
        up_sum, down_sum = call(
            join_kernel,
            [(odd, "scalar", None), whole(after(keep, held[2])), whole(got)],
            [fresh((rank, channels), f32), fresh((rank, channels), f32)],
            name="join",
        )
    else:
        u = exchange_pair(u_part, ("fsdp", "head"))
        adapter_output, up_part = call(
            adapter_kernel,
            [*map(whole, u), whole(adapter_up_map), whole(layer_output_gradient)],
            [fresh((length, channels), bf16), fresh((rank, channels), f32)],
            cost=1.5,
            name="adapter",
        )
        for g in everything:
            c_grad, *pair = pair_call(g, c_grad)
            pairs.append(pair)
            leaving = chain(state_grads[g], decays[g], "ctx", True)
            *held, _ = input_call(g, leaving, held, decays[g])
        up_sum = exchange_sum(up_part, ("ctx",))
        down_sum = exchange_sum(down_part, ("ctx",))
    x_grad, b_grad, step_grad = held
    return (
        mixed,
        adapter_output,
        x_grad,
        gate_grad,
        b_grad,
        c_grad,
        step_grad,
        down_sum.T,
        up_sum,
    )


def solution(mesh):
    rows_cols = P(("parts", "ctx"), ("head", "fsdp"))
    heads = P(("head", "fsdp"))
    in_specs = (
        rows_cols,
        rows_cols,
        rows_cols,
        rows_cols,
        P(("head", "fsdp"), ("parts", "ctx")),
        P(("parts", "ctx")),
        heads,
        heads,
        heads,
        heads,
        P(("head", "fsdp"), None),
        P(None, ("head", "fsdp")),
        rows_cols,
        rows_cols,
    )
    out_specs = (
        rows_cols,
        rows_cols,
        rows_cols,
        rows_cols,
        rows_cols,
        rows_cols,
        P(("head", "fsdp"), ("parts", "ctx")),
        P(("parts", "head", "fsdp"), None),
        P("parts", ("head", "fsdp")),
    )
    return jax.shard_map(
        per_device, mesh=mesh, in_specs=in_specs, out_specs=out_specs, check_vma=False
    )
```

```python
import functools

import jax
import jax.numpy as jnp
from jax import lax
from jax.experimental import pallas as pl
from jax.experimental.pallas import tpu as pltpu
from jax.sharding import PartitionSpec as P

STATE = 128
HEAD = 64
ROWS = 32
EPS = 1e-05
SCALE = 2.0
VMEM = 18 * 2**20
COST = 3.69e6

f32 = jnp.float32
bf16 = jnp.bfloat16


def dot(left, right, left_dim, right_dim):
    return lax.dot_general(
        left, right, (((left_dim,), (right_dim,)), ((), ())), preferred_element_type=f32
    )


def split2(v):
    high = v.astype(bf16)
    return high, (v - high.astype(f32)).astype(bf16)


def split3(v):
    high = v.astype(bf16)
    rest = v - high.astype(f32)
    mid = rest.astype(bf16)
    return high, mid, (rest - mid.astype(f32)).astype(bf16)


def head_places(heads, channels):
    lane = lax.broadcasted_iota(jnp.int32, (heads, channels), 1)
    row = lax.broadcasted_iota(jnp.int32, (heads, channels), 0)
    return lane // HEAD == row


def spread(v, places):
    ones = places.astype(bf16)
    return dot(
        jnp.concatenate(split2(v), axis=0), jnp.concatenate([ones, ones], axis=0), 0, 0
    )


def head_column(row, heads, first):
    lane = lax.broadcasted_iota(jnp.int32, (heads, row.shape[1]), 1)
    place = lax.broadcasted_iota(jnp.int32, (heads, row.shape[1]), 0)
    return jnp.sum(jnp.where(lane == place + first, row, 0.0), axis=1, keepdims=True)


def spread_row(v, places):
    return jnp.sum(jnp.where(places, v, 0.0), axis=0, keepdims=True)


def running_sum(v, exclusive):
    rows, length = v.shape
    s = lax.broadcasted_iota(jnp.int32, (length, length), 0)
    r = lax.broadcasted_iota(jnp.int32, (length, length), 1)
    upper = ((s < r) if exclusive else (s <= r)).astype(bf16)
    sums = dot(jnp.concatenate(split3(v), axis=0), upper, 1, 0)
    return sums[:rows] + sums[rows : 2 * rows] + sums[2 * rows :]


def state_kernel(
    x, b, c, step, resets, rates, biases, xw, state, bend, cstart, small, rows, ids_row, ids_col, first
):
    heads, length = step.shape
    rate = head_column(rates[...], heads, first)
    bias = head_column(biases[...], heads, first)
    channels = x.shape[1]
    places = head_places(heads, channels)
    raw = step[...] + bias
    dt = jnp.maximum(raw, 0.0) + jnp.log1p(jnp.exp(-jnp.abs(raw)))
    log_step = -rate * dt
    s = lax.broadcasted_iota(jnp.int32, (length, length), 0)
    r = lax.broadcasted_iota(jnp.int32, (length, length), 1)
    upper = (s <= r).astype(bf16)
    lower = (s >= r).astype(bf16)
    marks = jnp.broadcast_to(resets[...].astype(f32), (8, length)).astype(bf16)
    sums = dot(jnp.concatenate((marks,) + split3(log_step), axis=0), upper, 1, 0)
    ids = sums[:8]
    cum = sums[8 : 8 + heads] + sums[8 + heads : 8 + 2 * heads] + sums[8 + 2 * heads :]
    id_cols = dot(lower, marks, 1, 1)
    ids_row[...] = ids
    ids_col[...] = id_cols
    last = cum[:, length - 1 :]
    last_id = ids[:1, length - 1 :]
    middle = 0.5 * last
    fall = jnp.exp(cum - middle)
    rise = jnp.exp(middle - cum)
    weight = dt * rise
    small[0:heads] = dt
    small[heads : 2 * heads] = fall
    small[2 * heads : 3 * heads] = rise
    small[3 * heads :] = raw
    half_row = spread_row(jnp.exp(middle), places)
    total = jnp.where(last_id == 0, half_row * half_row, 0.0)
    rows[0:1] = total
    rows[1:2] = half_row
    rows[2:8] = jnp.zeros((6, channels), f32)
    xw[...] = (x[...].astype(f32) * spread(weight, places)).astype(bf16)
    to_end = id_cols[:, :1] == last_id
    from_start = id_cols[:, :1] == 0
    bend[...] = jnp.where(to_end, b[...].astype(f32), 0.0).astype(bf16)
    cstart[...] = jnp.where(from_start, c[...].astype(f32), 0.0).astype(bf16)
    state[...] = dot(bend[...], xw[...], 0, 0) * half_row


def score_kernel(b, c, ids_row, ids_col, xw, y_loc):
    length = b.shape[0]
    half = length // 2
    for i in range(2):
        here = pl.ds(i * half, half)
        total = None
        for j in range(i + 1):
            there = pl.ds(j * half, half)
            scores = dot(c[here], b[there], 1, 1)
            same = ids_col[here, 0:1] == ids_row[0:1, there]
            if i == j:
                r = lax.broadcasted_iota(jnp.int32, (half, half), 0)
                s = lax.broadcasted_iota(jnp.int32, (half, half), 1)
                same = same & (r >= s)
            m = jnp.where(same, scores, 0.0).astype(bf16)
            term = dot(m, xw[there], 1, 0)
            total = term if total is None else total + term
        y_loc[here] = total


def gather_incoming(near, far, mid):
    return near[...] + far[...] + mid[...]


def norm_kernel(*refs, first):
    refs = list(refs)
    (y_loc, cstart, near, far, mid, small, rows, x, gate, skips, gain, frozen) = refs[:12]
    (gu_here, gu_there, down) = refs[12:15]
    refs = refs[15:]
    u_before = None if first == 0 else refs.pop(0)
    (mixed, gate_grad, down_part, gye, scaled, state_grad, u_part, y_dot, decay) = refs[:9]
    (inner, falls, g_mixed, product) = refs[9:]
    decay[...] = rows[0:1]
    length, channels = x.shape
    heads = channels // HEAD
    skip = head_column(skips[...], heads, first)
    gu = (SCALE * (gu_here[...] + gu_there[...])).astype(bf16)
    places = head_places(heads, channels)
    scaled[...] = (gather_incoming(near, far, mid) * rows[1:2]).astype(bf16)
    inner[...] = y_loc[...] + dot(cstart[...], scaled[...], 1, 0)
    falls[...] = spread(small[heads : 2 * heads], places)
    g_mixed[...] = dot(gu, down[...], 0, 0)
    skip_row = spread_row(skip, places)
    gain_row = gain[...]

    def tile(i, carry):
        at = pl.ds(pl.multiple_of(i * ROWS, ROWS), ROWS)
        fall = falls[at]
        within = inner[at]
        z = gate[at].astype(f32)
        y = fall * within + skip_row * x[at].astype(f32)
        sig = 0.5 * jnp.tanh(0.5 * z) + 0.5
        act = z * sig
        grouped = y * act
        inv = lax.rsqrt(jnp.sum(grouped * grouped, axis=1, keepdims=True) * (1.0 / channels) + EPS)
        normed = grouped * inv
        mixed[at] = (normed * gain_row).astype(bf16)
        g_norm = (frozen[at].astype(f32) + g_mixed[at]) * gain_row
        mean = jnp.sum(g_norm * normed, axis=1, keepdims=True) * (1.0 / channels)
        g_grouped = inv * (g_norm - normed * mean)
        gate_grad[at] = (g_grouped * y * (sig + act * (1.0 - sig))).astype(bf16)
        g = (g_grouped * act * fall).astype(bf16)
        gye[at] = g
        high, low = split2(g.astype(f32) * within)
        product[0, at] = high
        product[1, at] = low
        return carry

    lax.fori_loop(0, length // ROWS, tile, 0, unroll=length // ROWS)
    state_grad[...] = dot(cstart[...], gye[...], 0, 0) * rows[1:2]
    u_here = dot(down[...], mixed[...], 1, 1)
    u_part[...] = u_here if first == 0 else u_here + u_before[...]
    down_part[...] = dot(gu, mixed[...], 1, 0)
    ones = places.astype(bf16)
    y_dot[...] = dot(ones, product[0], 1, 1) + dot(ones, product[1], 1, 1)


def pair_kernel(b, c, ids_row, ids_col, xw, gye, scaled_in, c_grad, z_loc, b_loc):
    length = b.shape[0]
    half = length // 2
    scaled = scaled_in[...]
    for i in range(2):
        here = pl.ds(i * half, half)
        carried = dot(gye[here], scaled, 1, 1)
        total = jnp.where(ids_col[here, 0:1] == 0, carried, 0.0)
        for j in range(i + 1):
            there = pl.ds(j * half, half)
            same = ids_col[here, 0:1] == ids_row[0:1, there]
            if i == j:
                r = lax.broadcasted_iota(jnp.int32, (half, half), 0)
                s = lax.broadcasted_iota(jnp.int32, (half, half), 1)
                same = same & (r >= s)
            pair = jnp.where(same, dot(gye[here], xw[there], 1, 1), 0.0).astype(bf16)
            total += dot(pair, b[there], 1, 0)
        c_grad[here] = total.astype(bf16)
    for j in range(2):
        there = pl.ds(j * half, half)
        z_total = None
        for i in range(j, 2):
            here = pl.ds(i * half, half)
            same = ids_col[there, 0:1] == ids_row[0:1, here]
            if i == j:
                s = lax.broadcasted_iota(jnp.int32, (half, half), 0)
                r = lax.broadcasted_iota(jnp.int32, (half, half), 1)
                same = same & (r >= s)
            m = jnp.where(same, dot(b[there], c[here], 1, 1), 0.0).astype(bf16)
            pair = jnp.where(same, dot(xw[there], gye[here], 1, 1), 0.0).astype(bf16)
            z_term = dot(m, gye[here], 1, 0)
            b_term = dot(pair, c[here], 1, 0)
            z_total = z_term if z_total is None else z_total + z_term
            b_total = b_term if i == j else b_total + b_term
        z_loc[there] = z_total
        b_loc[there] = b_total


def input_kernel(
    z_loc, b_loc, bend, ids_col, ids_row, xw, gye, near, far, mid, grad_dev, scaled_in, rows, small, skips,
    rates, y_dot, passing,
    x_grad, b_grad, step_grad, passed,
    inner, weights, rises, product,
    first,
):
    length, channels = xw.shape
    heads = channels // HEAD
    skip = head_column(skips[...], heads, first)
    rate = head_column(rates[...], heads, first)
    places = head_places(heads, channels)
    dt = small[0:heads]
    rise = small[2 * heads : 3 * heads]
    raw = small[3 * heads :]
    incoming = gather_incoming(near, far, mid)
    passed[...] = passing[...]
    scaled = (incoming * rows[1:2]).astype(bf16)
    inner[...] = z_loc[...] + dot(bend[...], scaled, 1, 0)
    weights[...] = spread(dt * rise, places)
    rises[...] = spread(skip * rise, places)

    def tile(i, carry):
        at = pl.ds(pl.multiple_of(i * ROWS, ROWS), ROWS)
        z = inner[at]
        x_grad[at] = (weights[at] * z + rises[at] * gye[at].astype(f32)).astype(bf16)
        high, low = split2(xw[at].astype(f32) * z)
        product[0, at] = high
        product[1, at] = low
        return carry

    lax.fori_loop(0, length // ROWS, tile, 0, unroll=length // ROWS)
    carried = dot(xw[...], scaled, 1, 1)
    to_end = ids_col[:, 0:1] == ids_row[0:1, length - 1 :]
    b_grad[...] = (b_loc[...] + jnp.where(to_end, carried, 0.0)).astype(bf16)
    ones = places.astype(bf16)
    x_dot = dot(ones, product[0], 1, 1) + dot(ones, product[1], 1, 1)
    crossing = jnp.sum(
        (rows[0:1] * incoming + grad_dev[...]) * scaled_in[...].astype(f32), axis=0, keepdims=True
    ) / rows[1:2]
    constant = jnp.sum(jnp.where(places, crossing, 0.0), axis=1, keepdims=True)
    g_log = running_sum(x_dot - y_dot[...], True) + constant
    g_dt = x_dot / dt - rate * g_log
    step_grad[...] = g_dt / (1.0 + jnp.exp(-raw))


def adapter_kernel(u_here, u_there, up, lo, out, up_part):
    u = (SCALE * (u_here[...] + u_there[...])).astype(bf16)
    out[...] = dot(u, up[...], 0, 0).astype(bf16)
    up_part[...] = dot(u, lo[...], 1, 0)


def output_kernel(u, up, out):
    out[...] = dot(u[...], up[...], 0, 0).astype(bf16)


def halves_kernel(odd, u_here, u_there, lo, down_part, u_out, keep, send):
    u = (SCALE * (u_here[...] + u_there[...])).astype(bf16)
    u_out[...] = u
    rows = keep.shape[0] // 2
    is_odd = odd[0] == 1
    down = down_part[...]
    keep[rows:] = jnp.where(is_odd, down[rows:], down[:rows])
    send[rows:] = jnp.where(is_odd, down[:rows], down[rows:])
    up_part = dot(u, lo[...], 1, 0)
    keep[:rows] = jnp.where(is_odd, up_part[rows:], up_part[:rows])
    send[:rows] = jnp.where(is_odd, up_part[:rows], up_part[rows:])


def join_kernel(odd, keep, other, up_out, down_out):
    is_odd = odd[0] == 1
    rows = keep.shape[0] // 2
    for at, out in ((pl.ds(0, rows), up_out), (pl.ds(rows, rows), down_out)):
        out[:rows] = jnp.where(is_odd, other[at], keep[at])
        out[rows:] = jnp.where(is_odd, keep[at], other[at])


def rank_kernel(up, lo, part):
    part[...] = dot(up[...], lo[...], 1, 1)


def call(kernel, ins, outs, scratch=(), cost=1.0, name=None):
    in_specs, operands = [], []
    for array, block, index, *pinned in ins:
        if pinned:
            array = pltpu.with_memory_space_constraint(array, pltpu.HBM)
        if block in ("scalar", "far"):
            space = pltpu.SMEM if block == "scalar" else pltpu.HBM
            in_specs.append(pl.BlockSpec(memory_space=space))
            operands.append(array)
            continue
        if block is None:
            block, index = array.shape, (0,) * array.ndim
        in_specs.append(pl.BlockSpec(block, functools.partial(lambda at, i: at, index)))
        operands.append(array)
    out_specs, out_shapes, aliases = [], [], {}
    for at, (shape, dtype, block, index, held, *pinned) in enumerate(outs):
        if block is None:
            block, index = shape, (0,) * len(shape)
        out_specs.append(pl.BlockSpec(block, functools.partial(lambda at, i: at, index)))
        out_shapes.append((pltpu.HBM if pinned else jax.ShapeDtypeStruct)(shape, dtype))
        if held is not None:
            aliases[len(operands)] = at
            operands.append(held)
            in_specs.append(pl.BlockSpec(memory_space=pl.ANY))
    n_real = len(ins)
    n_held = len(operands) - n_real

    def body(*refs):
        kernel(*refs[:n_real], *refs[n_real + n_held :])

    return pl.pallas_call(
        body,
        grid=(1,),
        in_specs=in_specs,
        out_specs=out_specs,
        out_shape=out_shapes,
        scratch_shapes=list(scratch),
        input_output_aliases=aliases,
        compiler_params=pltpu.CompilerParams(vmem_limit_bytes=VMEM),
        cost_estimate=pl.CostEstimate(
            flops=0, bytes_accessed=int(cost * COST), transcendentals=0
        ),
        name=name,
    )(*operands)


def after(value, *others):
    return lax.optimization_barrier((value, *others))[0]


def hop(part, axis, *pairs):
    return lax.ppermute(part, axis, list(pairs))


def chain(state, decay, axis, reverse):
    count = lax.axis_size(axis)
    incoming = jnp.zeros_like(state)
    out = state
    for at in range(count - 1):
        got = hop(out, axis, (count - 1 - at, count - 2 - at) if reverse else (at, at + 1))
        incoming = incoming + got
        out = state + decay * got
    return incoming, jnp.zeros_like(state), jnp.zeros_like(state)


def exchange_pair(part, axes, *before):
    other = None
    for axis in axes:
        count = lax.axis_size(axis)
        span = 1
        while span < count:
            part = part if other is None else after(part, *before) + other
            other = lax.ppermute(part, axis, [(i, i ^ span) for i in range(count)])
            span *= 2
    return part, other


def exchange_sum(part, axes):
    here, there = exchange_pair(part, axes)
    return here + there


def per_device(
    mixer_input_channels,
    gate_channels,
    input_group_maps,
    output_group_maps,
    step_size_input,
    resets,
    head_decay_rate,
    step_size_bias,
    skip,
    gated_norm_gain,
    adapter_down_map,
    adapter_up_map,
    frozen_mixed_gradient,
    layer_output_gradient,
):
    length, channels = mixer_input_channels.shape
    groups = input_group_maps.shape[1] // STATE
    heads = step_size_input.shape[0] // groups
    width = channels // groups
    rank = adapter_up_map.shape[0]
    resets = resets.reshape(1, length)
    rates = head_decay_rate.reshape(1, -1)
    biases = step_size_bias.reshape(1, -1)
    skips = skip.reshape(1, -1)
    down_map = adapter_down_map.T
    gains = gated_norm_gain.reshape(1, -1)

    def cols(array, g):
        return (array, (array.shape[0], array.shape[1] // groups), (0, g))

    def head_rows(array, g):
        return (array, (heads, array.shape[1]), (g, 0))

    def whole(array):
        return (array, None, None)

    def fresh(shape, dtype):
        return (shape, dtype, None, None, None)

    def far(array):
        return (array, "far", None, True)

    def slow(item):
        return (*item, True)

    everything = range(groups)
    short = lax.axis_size("ctx") == 4

    def state_call(g, rates):
        return call(
            functools.partial(state_kernel, first=g * heads),
            [
                slow(cols(mixer_input_channels, g)),
                slow(cols(input_group_maps, g)),
                slow(cols(output_group_maps, g)),
                slow(head_rows(step_size_input, g)),
                slow(whole(resets)),
                slow(whole(rates)),
                slow(whole(biases)),
            ],
            [
                fresh((length, width), bf16),
                fresh((STATE, width), f32),
                slow(fresh((length, STATE), bf16)),
                fresh((length, STATE), bf16),
                fresh((4 * heads, length), f32),
                fresh((8, width), f32),
                fresh((8, length), f32),
                fresh((length, 8), f32),
            ],
            cost=1.5,
            name="state",
        )

    def score_call(g, *before):
        xw, _, _, _, _, _, ids_row, ids_col = states[g]
        ids_row = after(ids_row, *before) if before else ids_row
        return call(
            score_kernel,
            [
                cols(input_group_maps, g),
                cols(output_group_maps, g),
                whole(ids_row),
                whole(ids_col),
                whole(xw),
            ],
            [fresh((length, width), f32)],
            cost=1.0,
            name="score",
        )[0]

    def rank_call(*before):
        return call(
            rank_kernel,
            [
                whole(after(adapter_up_map, *before) if before else adapter_up_map),
                whole(layer_output_gradient),
            ],
            [fresh((rank, length), f32)],
            cost=1.0,
            name="rank",
        )[0]

    states, y_locs = [state_call(0, rates)], []
    gu_part = rank_call(states[0][5])
    for g in range(1, groups):
        states.append(state_call(g, after(rates, gu_part)))

    parts = [states[g][1] for g in everything]
    decays = [states[g][5][0:1] for g in everything]
    entering = []
    if short:
        first = [hop(parts[g], "ctx", (0, 1)) for g in everything]
        gu = exchange_pair(gu_part, ("fsdp", "head"), states[-1][5])
        y_locs.append(score_call(0, gu[0]))
        joined = [after(decays[g], y_locs[0]) * first[g] + parts[g] for g in everything]
        second = [hop(joined[g], "ctx", (1, 2)) for g in everything]
        joined = decays[0] * second[0] + parts[0]
        third = [hop(joined, "ctx", (2, 3))]
        for g in range(1, groups):
            y_locs.append(score_call(g, joined))
            joined = after(decays[g], y_locs[-1], gu[1]) * second[g] + parts[g]
            third.append(hop(joined, "ctx", (2, 3)))
        entering = list(zip(first, second, third))
    else:
        y_locs = [score_call(g) for g in everything]
        gu = exchange_pair(gu_part, ("fsdp", "head"))
        entering = [chain(parts[g], decays[g], "ctx", False) for g in everything]
    mixed = gate_grad = down_part = u_part = c_grad = None
    normed, pairs = [], []

    def pair_call(g, held, *others):
        xw, state, bend, cstart, small, rows, ids_row, ids_col = states[g]
        return call(
            pair_kernel,
            [
                cols(input_group_maps, g),
                cols(output_group_maps, g),
                whole(after(ids_row, *others) if others else ids_row),
                whole(ids_col),
                whole(xw),
                whole(normed[g][0]),
                whole(normed[g][1]),
            ],
            [
                ((length, groups * STATE), bf16, (length, STATE), (0, g), held),
                fresh((length, width), f32),
                fresh((length, STATE), f32),
            ],
            cost=2.0,
            name="pair",
        )

    for g in everything:
        xw, state, bend, cstart, small, rows, ids_row, ids_col = states[g]
        results = call(
            functools.partial(norm_kernel, first=g * heads),
            [
                whole(y_locs[g]),
                whole(cstart),
                *map(whole, entering[g]),
                whole(small),
                whole(rows),
                cols(mixer_input_channels, g),
                cols(gate_channels, g),
                whole(skips),
                cols(gains, g),
                cols(frozen_mixed_gradient, g),
                *map(whole, gu),
                cols(down_map, g),
            ]
            + ([] if g == 0 else [whole(u_part)]),
            [
                ((length, channels), bf16, (length, width), (0, g), mixed),
                ((length, channels), bf16, (length, width), (0, g), gate_grad),
                slow(((rank, channels), f32, (rank, width), (0, g), down_part)),
                (slow if g < groups - 1 else tuple)(fresh((length, width), bf16)),
                slow(fresh((STATE, width), bf16)),
                fresh((STATE, width), f32),
                fresh((rank, length), f32),
                slow(fresh((heads, length), f32)),
                fresh((1, width), f32),
            ],
            [
                pltpu.VMEM((length, width), f32),
                pltpu.VMEM((length, width), f32),
                pltpu.VMEM((length, width), f32),
                pltpu.VMEM((2, length, width), bf16),
            ],
            cost=4.0,
            name="norm",
        )
        mixed, gate_grad, down_part, gye, scaled, state_grad, u_part, y_dot, decay = results
        normed.append((gye, scaled, state_grad, y_dot, decay))
    def input_call(g, leaving, held, passing, *before):
        xw, state, bend, cstart, small, rows, ids_row, ids_col = states[g]
        x_grad, b_grad, step_grad = held
        return call(
            functools.partial(input_kernel, first=g * heads),
            [
                whole(pairs[g][0]),
                whole(pairs[g][1]),
                whole(bend),
                whole(ids_col),
                whole(ids_row),
                whole(xw),
                whole(normed[g][0]),
                *map(whole, leaving),
                whole(normed[g][2]),
                whole(normed[g][1]),
                whole(rows),
                whole(small),
                whole(skips),
                whole(after(rates, *before) if before else rates),
                slow(whole(normed[g][3])),
                whole(passing),
            ],
            [
                ((length, channels), bf16, (length, width), (0, g), x_grad),
                ((length, groups * STATE), bf16, (length, STATE), (0, g), b_grad),
                ((groups * heads, length), f32, (heads, length), (g, 0), step_grad),
                fresh(passing.shape, f32),
            ],
            [
                pltpu.VMEM((length, width), f32),
                pltpu.VMEM((length, width), f32),
                pltpu.VMEM((length, width), f32),
                pltpu.VMEM((2, length, width), bf16),
            ],
            cost=2.5,
            name="input",
        )

    state_grads = [normed[g][2] for g in everything]
    decays = [normed[g][4] for g in everything]
    held = (None, None, None)
    if short and groups == 2:
        neighbours = [(0, 1), (1, 0), (2, 3), (3, 2)]
        across = [(0, 2), (2, 0), (1, 3), (3, 1)]
        last = [hop(state_grads[g], "ctx", (3, 2)) for g in everything]
        sent = after(decays[0], u_part) * last[0] + state_grads[0]
        then = [hop(sent, "ctx", (2, 1))]
        u = exchange_pair(u_part, ("fsdp", "head"), sent)
        odd = (lax.axis_index("ctx") % 2).reshape(1)
        half = fresh((rank, channels), f32)
        u, keep, send = call(
            halves_kernel,
            [
                (odd, "scalar", None),
                *map(whole, u),
                whole(layer_output_gradient),
                slow(whole(down_part)),
            ],
            [fresh((rank, length), bf16), half, half],
            cost=1.5,
            name="halves",
        )
        sent = after(decays[1], keep) * last[1] + state_grads[1]
        then.append(hop(sent, "ctx", (2, 1)))
        got = hop(send, "ctx", *neighbours)
        sent = after(decays[0], sent) * then[0] + state_grads[0]
        ahead = [hop(sent, "ctx", (1, 0))]
        c_grad, *pair = pair_call(0, c_grad, sent)
        pairs.append(pair)
        sent = after(decays[1], pair[1]) * then[1] + state_grads[1]
        ahead.append(hop(sent, "ctx", (1, 0)))
        keep = after(keep, sent) + got
        got = hop(keep, "ctx", *across)
        c_grad, *pair = pair_call(1, c_grad, keep)
        pairs.append(pair)
        *held, _ = input_call(0, (last[0], then[0], ahead[0]), held, decays[1], pair[1])
        (adapter_output,) = call(
            output_kernel,
            [whole(after(u, pair[1])), whole(adapter_up_map)],
            [fresh((length, channels), bf16)],
            name="output",
        )
        keep = after(keep, held[2]) + got
        got = hop(keep, "ctx", *neighbours)
        *held, _ = input_call(1, (last[1], then[1], ahead[1]), held, decays[1])
        up_sum, down_sum = call(
            join_kernel,
            [(odd, "scalar", None), whole(after(keep, held[2])), whole(got)],
            [fresh((rank, channels), f32), fresh((rank, channels), f32)],
            name="join",
        )
    else:
        u = exchange_pair(u_part, ("fsdp", "head"))
        adapter_output, up_part = call(
            adapter_kernel,
            [*map(whole, u), whole(adapter_up_map), whole(layer_output_gradient)],
            [fresh((length, channels), bf16), fresh((rank, channels), f32)],
            cost=1.5,
            name="adapter",
        )
        for g in everything:
            c_grad, *pair = pair_call(g, c_grad)
            pairs.append(pair)
            leaving = chain(state_grads[g], decays[g], "ctx", True)
            *held, _ = input_call(g, leaving, held, decays[g])
        up_sum = exchange_sum(up_part, ("ctx",))
        down_sum = exchange_sum(down_part, ("ctx",))
    x_grad, b_grad, step_grad = held
    return (
        mixed,
        adapter_output,
        x_grad,
        gate_grad,
        b_grad,
        c_grad,
        step_grad,
        down_sum.T,
        up_sum,
    )


def solution(mesh):
    rows_cols = P(("parts", "ctx"), ("head", "fsdp"))
    heads = P(("head", "fsdp"))
    in_specs = (
        rows_cols,
        rows_cols,
        rows_cols,
        rows_cols,
        P(("head", "fsdp"), ("parts", "ctx")),
        P(("parts", "ctx")),
        heads,
        heads,
        heads,
        heads,
        P(("head", "fsdp"), None),
        P(None, ("head", "fsdp")),
        rows_cols,
        rows_cols,
    )
    out_specs = (
        rows_cols,
        rows_cols,
        rows_cols,
        rows_cols,
        rows_cols,
        rows_cols,
        P(("head", "fsdp"), ("parts", "ctx")),
        P(("parts", "head", "fsdp"), None),
        P("parts", ("head", "fsdp")),
    )
    return jax.shard_map(
        per_device, mesh=mesh, in_specs=in_specs, out_specs=out_specs, check_vma=False
    )
```

```python
import functools

import jax
import jax.numpy as jnp
from jax import lax
from jax.experimental import pallas as pl
from jax.experimental.pallas import tpu as pltpu
from jax.sharding import PartitionSpec as P

STATE = 128
HEAD = 64
ROWS = 32
EPS = 1e-05
SCALE = 2.0
VMEM = 18 * 2**20
COST = 3.69e6

f32 = jnp.float32
bf16 = jnp.bfloat16


def dot(left, right, left_dim, right_dim):
    return lax.dot_general(
        left, right, (((left_dim,), (right_dim,)), ((), ())), preferred_element_type=f32
    )


def split2(v):
    high = v.astype(bf16)
    return high, (v - high.astype(f32)).astype(bf16)


def split3(v):
    high = v.astype(bf16)
    rest = v - high.astype(f32)
    mid = rest.astype(bf16)
    return high, mid, (rest - mid.astype(f32)).astype(bf16)


def head_places(heads, channels):
    lane = lax.broadcasted_iota(jnp.int32, (heads, channels), 1)
    row = lax.broadcasted_iota(jnp.int32, (heads, channels), 0)
    return lane // HEAD == row


def spread(v, places):
    ones = places.astype(bf16)
    return dot(
        jnp.concatenate(split2(v), axis=0), jnp.concatenate([ones, ones], axis=0), 0, 0
    )


def head_column(row, heads, first):
    lane = lax.broadcasted_iota(jnp.int32, (heads, row.shape[1]), 1)
    place = lax.broadcasted_iota(jnp.int32, (heads, row.shape[1]), 0)
    return jnp.sum(jnp.where(lane == place + first, row, 0.0), axis=1, keepdims=True)


def spread_row(v, places):
    return jnp.sum(jnp.where(places, v, 0.0), axis=0, keepdims=True)


def running_sum(v, exclusive):
    rows, length = v.shape
    s = lax.broadcasted_iota(jnp.int32, (length, length), 0)
    r = lax.broadcasted_iota(jnp.int32, (length, length), 1)
    upper = ((s < r) if exclusive else (s <= r)).astype(bf16)
    sums = dot(jnp.concatenate(split3(v), axis=0), upper, 1, 0)
    return sums[:rows] + sums[rows : 2 * rows] + sums[2 * rows :]


def state_kernel(
    x, b, c, step, resets, rates, biases, xw, state, bend, cstart, small, rows, ids_row, ids_col, first
):
    heads, length = step.shape
    rate = head_column(rates[...], heads, first)
    bias = head_column(biases[...], heads, first)
    channels = x.shape[1]
    places = head_places(heads, channels)
    raw = step[...] + bias
    dt = jnp.maximum(raw, 0.0) + jnp.log1p(jnp.exp(-jnp.abs(raw)))
    log_step = -rate * dt
    s = lax.broadcasted_iota(jnp.int32, (length, length), 0)
    r = lax.broadcasted_iota(jnp.int32, (length, length), 1)
    upper = (s <= r).astype(bf16)
    lower = (s >= r).astype(bf16)
    marks = jnp.broadcast_to(resets[...].astype(f32), (8, length)).astype(bf16)
    sums = dot(jnp.concatenate((marks,) + split3(log_step), axis=0), upper, 1, 0)
    ids = sums[:8]
    cum = sums[8 : 8 + heads] + sums[8 + heads : 8 + 2 * heads] + sums[8 + 2 * heads :]
    id_cols = dot(lower, marks, 1, 1)
    ids_row[...] = ids
    ids_col[...] = id_cols
    last = cum[:, length - 1 :]
    last_id = ids[:1, length - 1 :]
    middle = 0.5 * last
    fall = jnp.exp(cum - middle)
    rise = jnp.exp(middle - cum)
    weight = dt * rise
    small[0:heads] = dt
    small[heads : 2 * heads] = fall
    small[2 * heads : 3 * heads] = rise
    small[3 * heads :] = raw
    half_row = spread_row(jnp.exp(middle), places)
    total = jnp.where(last_id == 0, half_row * half_row, 0.0)
    rows[0:1] = total
    rows[1:2] = half_row
    rows[2:8] = jnp.zeros((6, channels), f32)
    xw[...] = (x[...].astype(f32) * spread(weight, places)).astype(bf16)
    to_end = id_cols[:, :1] == last_id
    from_start = id_cols[:, :1] == 0
    bend[...] = jnp.where(to_end, b[...].astype(f32), 0.0).astype(bf16)
    cstart[...] = jnp.where(from_start, c[...].astype(f32), 0.0).astype(bf16)
    state[...] = dot(bend[...], xw[...], 0, 0) * half_row


def score_kernel(b, c, ids_row, ids_col, xw, y_loc):
    length = b.shape[0]
    half = length // 2
    for i in range(2):
        here = pl.ds(i * half, half)
        total = None
        for j in range(i + 1):
            there = pl.ds(j * half, half)
            scores = dot(c[here], b[there], 1, 1)
            same = ids_col[here, 0:1] == ids_row[0:1, there]
            if i == j:
                r = lax.broadcasted_iota(jnp.int32, (half, half), 0)
                s = lax.broadcasted_iota(jnp.int32, (half, half), 1)
                same = same & (r >= s)
            m = jnp.where(same, scores, 0.0).astype(bf16)
            term = dot(m, xw[there], 1, 0)
            total = term if total is None else total + term
        y_loc[here] = total


def gather_incoming(near, far, mid):
    return near[...] + far[...] + mid[...]


def split_rows(odd, part, keep, send):
    rows = keep.shape[0]
    is_odd = odd[0:1, 0:1] == 1
    keep[...] = jnp.where(is_odd, part[rows:], part[:rows])
    send[...] = jnp.where(is_odd, part[:rows], part[rows:])


def norm_kernel(odd, *refs, first):
    refs = list(refs)
    (y_loc, cstart, near, far, mid, small, rows, x, gate, skips, gain, frozen) = refs[:12]
    (gu_here, gu_there, down) = refs[12:15]
    refs = refs[15:]
    u_before = None if first == 0 else refs.pop(0)
    (mixed, gate_grad, keep, send, gye, scaled, state_grad, u_part, y_dot, decay) = refs[:10]
    (inner, falls, g_mixed, product) = refs[10:]
    decay[...] = rows[0:1]
    length, channels = x.shape
    heads = channels // HEAD
    skip = head_column(skips[...], heads, first)
    gu = (SCALE * (gu_here[...] + gu_there[...])).astype(bf16)
    places = head_places(heads, channels)
    scaled[...] = (gather_incoming(near, far, mid) * rows[1:2]).astype(bf16)
    inner[...] = y_loc[...] + dot(cstart[...], scaled[...], 1, 0)
    falls[...] = spread(small[heads : 2 * heads], places)
    g_mixed[...] = dot(gu, down[...], 0, 0)
    skip_row = spread_row(skip, places)
    gain_row = gain[...]

    def tile(i, carry):
        at = pl.ds(pl.multiple_of(i * ROWS, ROWS), ROWS)
        fall = falls[at]
        within = inner[at]
        z = gate[at].astype(f32)
        y = fall * within + skip_row * x[at].astype(f32)
        sig = 0.5 * jnp.tanh(0.5 * z) + 0.5
        act = z * sig
        grouped = y * act
        inv = lax.rsqrt(jnp.sum(grouped * grouped, axis=1, keepdims=True) * (1.0 / channels) + EPS)
        normed = grouped * inv
        mixed[at] = (normed * gain_row).astype(bf16)
        g_norm = (frozen[at].astype(f32) + g_mixed[at]) * gain_row
        mean = jnp.sum(g_norm * normed, axis=1, keepdims=True) * (1.0 / channels)
        g_grouped = inv * (g_norm - normed * mean)
        gate_grad[at] = (g_grouped * y * (sig + act * (1.0 - sig))).astype(bf16)
        g = (g_grouped * act * fall).astype(bf16)
        gye[at] = g
        high, low = split2(g.astype(f32) * within)
        product[0, at] = high
        product[1, at] = low
        return carry

    lax.fori_loop(0, length // ROWS, tile, 0, unroll=length // ROWS)
    state_grad[...] = dot(cstart[...], gye[...], 0, 0) * rows[1:2]
    u_here = dot(down[...], mixed[...], 1, 1)
    u_part[...] = u_here if first == 0 else u_here + u_before[...]
    down_part = dot(gu, mixed[...], 1, 0)
    split_rows(odd, down_part, keep, send)
    ones = places.astype(bf16)
    y_dot[...] = dot(ones, product[0], 1, 1) + dot(ones, product[1], 1, 1)


def pair_kernel(b, c, ids_row, ids_col, xw, gye, scaled_in, c_grad, z_loc, b_loc):
    length = b.shape[0]
    half = length // 2
    scaled = scaled_in[...]
    for i in range(2):
        here = pl.ds(i * half, half)
        carried = dot(gye[here], scaled, 1, 1)
        total = jnp.where(ids_col[here, 0:1] == 0, carried, 0.0)
        for j in range(i + 1):
            there = pl.ds(j * half, half)
            same = ids_col[here, 0:1] == ids_row[0:1, there]
            if i == j:
                r = lax.broadcasted_iota(jnp.int32, (half, half), 0)
                s = lax.broadcasted_iota(jnp.int32, (half, half), 1)
                same = same & (r >= s)
            pair = jnp.where(same, dot(gye[here], xw[there], 1, 1), 0.0).astype(bf16)
            total += dot(pair, b[there], 1, 0)
        c_grad[here] = total.astype(bf16)
    for j in range(2):
        there = pl.ds(j * half, half)
        z_total = None
        for i in range(j, 2):
            here = pl.ds(i * half, half)
            same = ids_col[there, 0:1] == ids_row[0:1, here]
            if i == j:
                s = lax.broadcasted_iota(jnp.int32, (half, half), 0)
                r = lax.broadcasted_iota(jnp.int32, (half, half), 1)
                same = same & (r >= s)
            m = jnp.where(same, dot(b[there], c[here], 1, 1), 0.0).astype(bf16)
            pair = jnp.where(same, dot(xw[there], gye[here], 1, 1), 0.0).astype(bf16)
            z_term = dot(m, gye[here], 1, 0)
            b_term = dot(pair, c[here], 1, 0)
            z_total = z_term if z_total is None else z_total + z_term
            b_total = b_term if i == j else b_total + b_term
        z_loc[there] = z_total
        b_loc[there] = b_total


def input_kernel(
    z_loc, b_loc, bend, ids_col, ids_row, xw, gye, near, far, mid, grad_dev, scaled_in, rows, small, skips,
    rates, y_dot, passing,
    x_grad, b_grad, step_grad, passed,
    inner, weights, rises, product,
    first,
):
    length, channels = xw.shape
    heads = channels // HEAD
    skip = head_column(skips[...], heads, first)
    rate = head_column(rates[...], heads, first)
    places = head_places(heads, channels)
    dt = small[0:heads]
    rise = small[2 * heads : 3 * heads]
    raw = small[3 * heads :]
    incoming = gather_incoming(near, far, mid)
    passed[...] = passing[...]
    scaled = (incoming * rows[1:2]).astype(bf16)
    inner[...] = z_loc[...] + dot(bend[...], scaled, 1, 0)
    weights[...] = spread(dt * rise, places)
    rises[...] = spread(skip * rise, places)

    def tile(i, carry):
        at = pl.ds(pl.multiple_of(i * ROWS, ROWS), ROWS)
        z = inner[at]
        x_grad[at] = (weights[at] * z + rises[at] * gye[at].astype(f32)).astype(bf16)
        high, low = split2(xw[at].astype(f32) * z)
        product[0, at] = high
        product[1, at] = low
        return carry

    lax.fori_loop(0, length // ROWS, tile, 0, unroll=length // ROWS)
    carried = dot(xw[...], scaled, 1, 1)
    to_end = ids_col[:, 0:1] == ids_row[0:1, length - 1 :]
    b_grad[...] = (b_loc[...] + jnp.where(to_end, carried, 0.0)).astype(bf16)
    ones = places.astype(bf16)
    x_dot = dot(ones, product[0], 1, 1) + dot(ones, product[1], 1, 1)
    crossing = jnp.sum(
        (rows[0:1] * incoming + grad_dev[...]) * scaled_in[...].astype(f32), axis=0, keepdims=True
    ) / rows[1:2]
    constant = jnp.sum(jnp.where(places, crossing, 0.0), axis=1, keepdims=True)
    g_log = running_sum(x_dot - y_dot[...], True) + constant
    g_dt = x_dot / dt - rate * g_log
    step_grad[...] = g_dt / (1.0 + jnp.exp(-raw))


def adapter_kernel(u_here, u_there, up, lo, out, up_part):
    u = (SCALE * (u_here[...] + u_there[...])).astype(bf16)
    out[...] = dot(u, up[...], 0, 0).astype(bf16)
    up_part[...] = dot(u, lo[...], 1, 0)


def output_kernel(u, up, out):
    out[...] = dot(u[...], up[...], 0, 0).astype(bf16)


def halves_kernel(
    odd, u_here, u_there, lo, keep_down, send_down, decay_in, u_out, keep, send, decay
):
    u = (SCALE * (u_here[...] + u_there[...])).astype(bf16)
    u_out[...] = u
    rows = keep_down.shape[0]
    split_rows(odd, dot(u, lo[...], 1, 0), keep.at[:rows], send.at[:rows])
    keep[rows:] = keep_down[...]
    send[rows:] = send_down[...]
    decay[...] = decay_in[...]


def join_kernel(odd, keep, got, up_out, down_out):
    is_odd = odd[0:1, 0:1] == 1
    rows = keep.shape[0] // 2
    for at, out in ((pl.ds(0, rows), up_out), (pl.ds(rows, rows), down_out)):
        out[:rows] = jnp.where(is_odd, got[at], keep[at])
        out[rows:] = jnp.where(is_odd, keep[at], got[at])


def rank_kernel(up, lo, odd, part, marks):
    marks[...] = odd[...]
    part[...] = dot(up[...], lo[...], 1, 1)


def call(kernel, ins, outs, scratch=(), cost=1.0, name=None):
    in_specs, operands = [], []
    for array, block, index, *pinned in ins:
        if pinned:
            array = pltpu.with_memory_space_constraint(array, pltpu.HBM)
        if block in ("scalar", "far"):
            space = pltpu.SMEM if block == "scalar" else pltpu.HBM
            in_specs.append(pl.BlockSpec(memory_space=space))
            operands.append(array)
            continue
        if block is None:
            block, index = array.shape, (0,) * array.ndim
        in_specs.append(pl.BlockSpec(block, functools.partial(lambda at, i: at, index)))
        operands.append(array)
    out_specs, out_shapes, aliases = [], [], {}
    for at, (shape, dtype, block, index, held, *pinned) in enumerate(outs):
        if block is None:
            block, index = shape, (0,) * len(shape)
        out_specs.append(pl.BlockSpec(block, functools.partial(lambda at, i: at, index)))
        out_shapes.append((pltpu.HBM if pinned else jax.ShapeDtypeStruct)(shape, dtype))
        if held is not None:
            aliases[len(operands)] = at
            operands.append(held)
            in_specs.append(pl.BlockSpec(memory_space=pl.ANY))
    n_real = len(ins)
    n_held = len(operands) - n_real

    def body(*refs):
        kernel(*refs[:n_real], *refs[n_real + n_held :])

    return pl.pallas_call(
        body,
        grid=(1,),
        in_specs=in_specs,
        out_specs=out_specs,
        out_shape=out_shapes,
        scratch_shapes=list(scratch),
        input_output_aliases=aliases,
        compiler_params=pltpu.CompilerParams(vmem_limit_bytes=VMEM),
        cost_estimate=pl.CostEstimate(
            flops=0, bytes_accessed=int(cost * COST), transcendentals=0
        ),
        name=name,
    )(*operands)


def after(value, *others):
    return lax.optimization_barrier((value, *others))[0]


def hop(part, axis, *pairs):
    return lax.ppermute(part, axis, list(pairs))


def chain(state, decay, axis, reverse):
    count = lax.axis_size(axis)
    incoming = jnp.zeros_like(state)
    out = state
    for at in range(count - 1):
        got = hop(out, axis, (count - 1 - at, count - 2 - at) if reverse else (at, at + 1))
        incoming = incoming + got
        out = state + decay * got
    return incoming, jnp.zeros_like(state), jnp.zeros_like(state)


def exchange_pair(part, axes, *before):
    other = None
    for axis in axes:
        count = lax.axis_size(axis)
        span = 1
        while span < count:
            part = part if other is None else after(part, *before) + other
            other = lax.ppermute(part, axis, [(i, i ^ span) for i in range(count)])
            span *= 2
    return part, other


def exchange_sum(part, axes):
    here, there = exchange_pair(part, axes)
    return here + there


def per_device(
    mixer_input_channels,
    gate_channels,
    input_group_maps,
    output_group_maps,
    step_size_input,
    resets,
    head_decay_rate,
    step_size_bias,
    skip,
    gated_norm_gain,
    adapter_down_map,
    adapter_up_map,
    frozen_mixed_gradient,
    layer_output_gradient,
):
    length, channels = mixer_input_channels.shape
    groups = input_group_maps.shape[1] // STATE
    heads = step_size_input.shape[0] // groups
    width = channels // groups
    rank = adapter_up_map.shape[0]
    resets = resets.reshape(1, length)
    rates = head_decay_rate.reshape(1, -1)
    biases = step_size_bias.reshape(1, -1)
    skips = skip.reshape(1, -1)
    down_map = adapter_down_map.T
    gains = gated_norm_gain.reshape(1, -1)

    def cols(array, g):
        return (array, (array.shape[0], array.shape[1] // groups), (0, g))

    def head_rows(array, g):
        return (array, (heads, array.shape[1]), (g, 0))

    def whole(array):
        return (array, None, None)

    def fresh(shape, dtype):
        return (shape, dtype, None, None, None)

    def far(array):
        return (array, "far", None, True)

    def slow(item):
        return (*item, True)

    everything = range(groups)
    short = lax.axis_size("ctx") == 4

    def state_call(g, rates):
        return call(
            functools.partial(state_kernel, first=g * heads),
            [
                slow(cols(mixer_input_channels, g)),
                slow(cols(input_group_maps, g)),
                slow(cols(output_group_maps, g)),
                slow(head_rows(step_size_input, g)),
                slow(whole(resets)),
                slow(whole(rates)),
                slow(whole(biases)),
            ],
            [
                fresh((length, width), bf16),
                fresh((STATE, width), f32),
                slow(fresh((length, STATE), bf16)),
                fresh((length, STATE), bf16),
                fresh((4 * heads, length), f32),
                fresh((8, width), f32),
                fresh((8, length), f32),
                fresh((length, 8), f32),
            ],
            cost=1.5,
            name="state",
        )

    def score_call(g, *before):
        xw, _, _, _, _, _, ids_row, ids_col = states[g]
        ids_row = after(ids_row, *before) if before else ids_row
        return call(
            score_kernel,
            [
                cols(input_group_maps, g),
                cols(output_group_maps, g),
                whole(ids_row),
                whole(ids_col),
                whole(xw),
            ],
            [fresh((length, width), f32)],
            cost=1.0,
            name="score",
        )[0]

    paired = short and groups == 2
    odd = jnp.full((8, 128), lax.axis_index("ctx") % 2 if paired else 0, jnp.int32)

    def rank_call(*before):
        return call(
            rank_kernel,
            [
                whole(after(adapter_up_map, *before) if before else adapter_up_map),
                whole(layer_output_gradient),
                whole(odd),
            ],
            [fresh((rank, length), f32), fresh((8, 128), jnp.int32)],
            cost=1.0,
            name="rank",
        )

    states, y_locs = [state_call(0, rates)], []
    gu_part, marks = rank_call(states[0][5])
    for g in range(1, groups):
        states.append(state_call(g, after(rates, gu_part)))

    parts = [states[g][1] for g in everything]
    decays = [states[g][5][0:1] for g in everything]
    entering = []
    if short:
        first = [hop(parts[g], "ctx", (0, 1)) for g in everything]
        gu = exchange_pair(gu_part, ("fsdp", "head"), states[-1][5])
        y_locs.append(score_call(0, gu[0]))
        joined = [after(decays[g], y_locs[0]) * first[g] + parts[g] for g in everything]
        second = [hop(joined[g], "ctx", (1, 2)) for g in everything]
        joined = decays[0] * second[0] + parts[0]
        third = [hop(joined, "ctx", (2, 3))]
        for g in range(1, groups):
            y_locs.append(score_call(g, joined))
            joined = after(decays[g], y_locs[-1], gu[1]) * second[g] + parts[g]
            third.append(hop(joined, "ctx", (2, 3)))
        entering = list(zip(first, second, third))
    else:
        y_locs = [score_call(g) for g in everything]
        gu = exchange_pair(gu_part, ("fsdp", "head"))
        entering = [chain(parts[g], decays[g], "ctx", False) for g in everything]
    mixed = gate_grad = keep_down = send_down = u_part = c_grad = None
    normed, pairs = [], []

    def pair_call(g, held, *others):
        xw, state, bend, cstart, small, rows, ids_row, ids_col = states[g]
        return call(
            pair_kernel,
            [
                cols(input_group_maps, g),
                cols(output_group_maps, g),
                whole(after(ids_row, *others) if others else ids_row),
                whole(ids_col),
                whole(xw),
                whole(normed[g][0]),
                whole(normed[g][1]),
            ],
            [
                ((length, groups * STATE), bf16, (length, STATE), (0, g), held),
                fresh((length, width), f32),
                fresh((length, STATE), f32),
            ],
            cost=2.0,
            name="pair",
        )

    for g in everything:
        xw, state, bend, cstart, small, rows, ids_row, ids_col = states[g]
        results = call(
            functools.partial(norm_kernel, first=g * heads),
            [
                whole(marks),
                whole(y_locs[g]),
                whole(cstart),
                *map(whole, entering[g]),
                whole(small),
                whole(rows),
                cols(mixer_input_channels, g),
                cols(gate_channels, g),
                whole(skips),
                cols(gains, g),
                cols(frozen_mixed_gradient, g),
                *map(whole, gu),
                cols(down_map, g),
            ]
            + ([] if g == 0 else [whole(u_part)]),
            [
                ((length, channels), bf16, (length, width), (0, g), mixed),
                ((length, channels), bf16, (length, width), (0, g), gate_grad),
                slow(((rank // 2, channels), f32, (rank // 2, width), (0, g), keep_down)),
                slow(((rank // 2, channels), f32, (rank // 2, width), (0, g), send_down)),
                (slow if g < groups - 1 else tuple)(fresh((length, width), bf16)),
                slow(fresh((STATE, width), bf16)),
                fresh((STATE, width), f32),
                fresh((rank, length), f32),
                slow(fresh((heads, length), f32)),
                (slow if g == groups - 1 else tuple)(fresh((1, width), f32)),
            ],
            [
                pltpu.VMEM((length, width), f32),
                pltpu.VMEM((length, width), f32),
                pltpu.VMEM((length, width), f32),
                pltpu.VMEM((2, length, width), bf16),
            ],
            cost=4.0,
            name="norm",
        )
        mixed, gate_grad, keep_down, send_down, gye, scaled, state_grad, u_part, y_dot, decay = results
        normed.append((gye, scaled, state_grad, y_dot, decay))
    def input_call(g, leaving, held, passing, *before):
        xw, state, bend, cstart, small, rows, ids_row, ids_col = states[g]
        x_grad, b_grad, step_grad = held
        return call(
            functools.partial(input_kernel, first=g * heads),
            [
                whole(pairs[g][0]),
                whole(pairs[g][1]),
                whole(bend),
                whole(ids_col),
                whole(ids_row),
                whole(xw),
                whole(normed[g][0]),
                *map(whole, leaving),
                whole(normed[g][2]),
                whole(normed[g][1]),
                whole(rows),
                whole(small),
                whole(skips),
                whole(after(rates, *before) if before else rates),
                slow(whole(normed[g][3])),
                whole(passing),
            ],
            [
                ((length, channels), bf16, (length, width), (0, g), x_grad),
                ((length, groups * STATE), bf16, (length, STATE), (0, g), b_grad),
                ((groups * heads, length), f32, (heads, length), (g, 0), step_grad),
                fresh(passing.shape, f32),
            ],
            [
                pltpu.VMEM((length, width), f32),
                pltpu.VMEM((length, width), f32),
                pltpu.VMEM((length, width), f32),
                pltpu.VMEM((2, length, width), bf16),
            ],
            cost=2.5,
            name="input",
        )

    state_grads = [normed[g][2] for g in everything]
    decays = [normed[g][4] for g in everything]
    held = (None, None, None)
    if paired:
        neighbours = [(0, 1), (1, 0), (2, 3), (3, 2)]
        across = [(0, 2), (2, 0), (1, 3), (3, 1)]
        last = [hop(state_grads[g], "ctx", (3, 2)) for g in everything]
        sent = after(decays[0], u_part) * last[0] + state_grads[0]
        then = [hop(sent, "ctx", (2, 1))]
        u = exchange_pair(u_part, ("fsdp", "head"), sent)
        half = fresh((rank, channels), f32)
        u, keep, send, decay = call(
            halves_kernel,
            [
                whole(odd),
                *map(whole, u),
                whole(layer_output_gradient),
                slow(whole(keep_down)),
                slow(whole(send_down)),
                slow(whole(decays[1])),
            ],
            [fresh((rank, length), bf16), half, half, fresh((1, width), f32)],
            cost=1.5,
            name="halves",
        )
        sent = decay * last[1] + state_grads[1]
        then.append(hop(sent, "ctx", (2, 1)))
        got = hop(send, "ctx", *neighbours)
        sent = after(decays[0], sent) * then[0] + state_grads[0]
        ahead = [hop(sent, "ctx", (1, 0))]
        c_grad, *pair = pair_call(0, c_grad, sent)
        pairs.append(pair)
        sent = after(decay, pair[1]) * then[1] + state_grads[1]
        ahead.append(hop(sent, "ctx", (1, 0)))
        keep = after(keep, sent) + got
        got = hop(keep, "ctx", *across)
        c_grad, *pair = pair_call(1, c_grad, keep)
        pairs.append(pair)
        *held, _ = input_call(0, (last[0], then[0], ahead[0]), held, decay, pair[1])
        (adapter_output,) = call(
            output_kernel,
            [whole(after(u, pair[1])), whole(adapter_up_map)],
            [fresh((length, channels), bf16)],
            name="output",
        )
        keep = after(keep, held[2]) + got
        got = hop(keep, "ctx", *neighbours)
        *held, _ = input_call(1, (last[1], then[1], ahead[1]), held, decay)
        up_sum, down_sum = call(
            join_kernel,
            [whole(odd), whole(after(keep, held[2])), whole(got)],
            [fresh((rank, channels), f32), fresh((rank, channels), f32)],
            name="join",
        )
    else:
        u = exchange_pair(u_part, ("fsdp", "head"))
        adapter_output, up_part = call(
            adapter_kernel,
            [*map(whole, u), whole(adapter_up_map), whole(layer_output_gradient)],
            [fresh((length, channels), bf16), fresh((rank, channels), f32)],
            cost=1.5,
            name="adapter",
        )
        for g in everything:
            c_grad, *pair = pair_call(g, c_grad)
            pairs.append(pair)
            leaving = chain(state_grads[g], decays[g], "ctx", True)
            *held, _ = input_call(g, leaving, held, decays[g])
        up_sum = exchange_sum(up_part, ("ctx",))
        down_sum = exchange_sum(jnp.concatenate([keep_down, send_down], axis=0), ("ctx",))
    x_grad, b_grad, step_grad = held
    return (
        mixed,
        adapter_output,
        x_grad,
        gate_grad,
        b_grad,
        c_grad,
        step_grad,
        down_sum.T,
        up_sum,
    )


def solution(mesh):
    rows_cols = P(("parts", "ctx"), ("head", "fsdp"))
    heads = P(("head", "fsdp"))
    in_specs = (
        rows_cols,
        rows_cols,
        rows_cols,
        rows_cols,
        P(("head", "fsdp"), ("parts", "ctx")),
        P(("parts", "ctx")),
        heads,
        heads,
        heads,
        heads,
        P(("head", "fsdp"), None),
        P(None, ("head", "fsdp")),
        rows_cols,
        rows_cols,
    )
    out_specs = (
        rows_cols,
        rows_cols,
        rows_cols,
        rows_cols,
        rows_cols,
        rows_cols,
        P(("head", "fsdp"), ("parts", "ctx")),
        P(("parts", "head", "fsdp"), None),
        P("parts", ("head", "fsdp")),
    )
    return jax.shard_map(
        per_device, mesh=mesh, in_specs=in_specs, out_specs=out_specs, check_vma=False
    )
```

```python
import functools

import jax
import jax.numpy as jnp
from jax import lax
from jax.experimental import pallas as pl
from jax.experimental.pallas import tpu as pltpu
from jax.sharding import PartitionSpec as P

STATE = 128
HEAD = 64
ROWS = 32
EPS = 1e-05
SCALE = 2.0
VMEM = 18 * 2**20
COST = 3.69e6

f32 = jnp.float32
bf16 = jnp.bfloat16


def dot(left, right, left_dim, right_dim):
    return lax.dot_general(
        left, right, (((left_dim,), (right_dim,)), ((), ())), preferred_element_type=f32
    )


def split2(v):
    high = v.astype(bf16)
    return high, (v - high.astype(f32)).astype(bf16)


def split3(v):
    high = v.astype(bf16)
    rest = v - high.astype(f32)
    mid = rest.astype(bf16)
    return high, mid, (rest - mid.astype(f32)).astype(bf16)


def head_places(heads, channels):
    lane = lax.broadcasted_iota(jnp.int32, (heads, channels), 1)
    row = lax.broadcasted_iota(jnp.int32, (heads, channels), 0)
    return lane // HEAD == row


def spread(v, places):
    ones = places.astype(bf16)
    return dot(
        jnp.concatenate(split2(v), axis=0), jnp.concatenate([ones, ones], axis=0), 0, 0
    )


def head_column(row, heads, first):
    lane = lax.broadcasted_iota(jnp.int32, (heads, row.shape[1]), 1)
    place = lax.broadcasted_iota(jnp.int32, (heads, row.shape[1]), 0)
    return jnp.sum(jnp.where(lane == place + first, row, 0.0), axis=1, keepdims=True)


def spread_row(v, places):
    return jnp.sum(jnp.where(places, v, 0.0), axis=0, keepdims=True)


def running_sum(v, exclusive):
    rows, length = v.shape
    s = lax.broadcasted_iota(jnp.int32, (length, length), 0)
    r = lax.broadcasted_iota(jnp.int32, (length, length), 1)
    upper = ((s < r) if exclusive else (s <= r)).astype(bf16)
    sums = dot(jnp.concatenate(split3(v), axis=0), upper, 1, 0)
    return sums[:rows] + sums[rows : 2 * rows] + sums[2 * rows :]


def state_kernel(
    x, b, c, step, resets, rates, biases, xw, state, bend, cstart, small, rows, ids_row, ids_col, first
):
    heads, length = step.shape
    rate = head_column(rates[...], heads, first)
    bias = head_column(biases[...], heads, first)
    channels = x.shape[1]
    places = head_places(heads, channels)
    raw = step[...] + bias
    dt = jnp.maximum(raw, 0.0) + jnp.log1p(jnp.exp(-jnp.abs(raw)))
    log_step = -rate * dt
    s = lax.broadcasted_iota(jnp.int32, (length, length), 0)
    r = lax.broadcasted_iota(jnp.int32, (length, length), 1)
    upper = (s <= r).astype(bf16)
    lower = (s >= r).astype(bf16)
    marks = jnp.broadcast_to(resets[...].astype(f32), (8, length)).astype(bf16)
    sums = dot(jnp.concatenate((marks,) + split3(log_step), axis=0), upper, 1, 0)
    ids = sums[:8]
    cum = sums[8 : 8 + heads] + sums[8 + heads : 8 + 2 * heads] + sums[8 + 2 * heads :]
    id_cols = dot(lower, marks, 1, 1)
    ids_row[...] = ids
    ids_col[...] = id_cols
    last = cum[:, length - 1 :]
    last_id = ids[:1, length - 1 :]
    middle = 0.5 * last
    fall = jnp.exp(cum - middle)
    rise = jnp.exp(middle - cum)
    weight = dt * rise
    small[0:heads] = dt
    small[heads : 2 * heads] = fall
    small[2 * heads : 3 * heads] = rise
    small[3 * heads :] = raw
    half_row = spread_row(jnp.exp(middle), places)
    total = jnp.where(last_id == 0, half_row * half_row, 0.0)
    rows[0:1] = total
    rows[1:2] = half_row
    rows[2:8] = jnp.zeros((6, channels), f32)
    xw[...] = (x[...].astype(f32) * spread(weight, places)).astype(bf16)
    to_end = id_cols[:, :1] == last_id
    from_start = id_cols[:, :1] == 0
    bend[...] = jnp.where(to_end, b[...].astype(f32), 0.0).astype(bf16)
    cstart[...] = jnp.where(from_start, c[...].astype(f32), 0.0).astype(bf16)
    state[...] = dot(bend[...], xw[...], 0, 0) * half_row


def score_kernel(b, c, ids_row, ids_col, xw, y_loc):
    length = b.shape[0]
    half = length // 2
    for i in range(2):
        here = pl.ds(i * half, half)
        total = None
        for j in range(i + 1):
            there = pl.ds(j * half, half)
            scores = dot(c[here], b[there], 1, 1)
            same = ids_col[here, 0:1] == ids_row[0:1, there]
            if i == j:
                r = lax.broadcasted_iota(jnp.int32, (half, half), 0)
                s = lax.broadcasted_iota(jnp.int32, (half, half), 1)
                same = same & (r >= s)
            m = jnp.where(same, scores, 0.0).astype(bf16)
            term = dot(m, xw[there], 1, 0)
            total = term if total is None else total + term
        y_loc[here] = total


def gather_incoming(near, far, mid):
    return near[...] + far[...] + mid[...]


def split_rows(odd, part, keep, send):
    rows = keep.shape[0]
    is_odd = odd[0:1, 0:1] == 1
    keep[...] = jnp.where(is_odd, part[rows:], part[:rows])
    send[...] = jnp.where(is_odd, part[:rows], part[rows:])


def norm_kernel(odd, *refs, first):
    refs = list(refs)
    (y_loc, cstart, near, far, mid, small, rows, x, gate, skips, gain, frozen) = refs[:12]
    (gu_here, gu_there, down) = refs[12:15]
    refs = refs[15:]
    u_before = None if first == 0 else refs.pop(0)
    (mixed, gate_grad, keep, send, gye, scaled, state_grad, u_part, y_dot, decay, gye_low) = refs[:11]
    (inner, falls, g_mixed, product) = refs[11:]
    decay[...] = rows[0:1]
    length, channels = x.shape
    heads = channels // HEAD
    skip = head_column(skips[...], heads, first)
    gu = (SCALE * (gu_here[...] + gu_there[...])).astype(bf16)
    places = head_places(heads, channels)
    scaled[...] = (gather_incoming(near, far, mid) * rows[1:2]).astype(bf16)
    inner[...] = y_loc[...] + dot(cstart[...], scaled[...], 1, 0)
    falls[...] = spread(small[heads : 2 * heads], places)
    g_mixed[...] = dot(gu, down[...], 0, 0)
    skip_row = spread_row(skip, places)
    gain_row = gain[...]

    def tile(i, carry):
        at = pl.ds(pl.multiple_of(i * ROWS, ROWS), ROWS)
        fall = falls[at]
        within = inner[at]
        z = gate[at].astype(f32)
        y = fall * within + skip_row * x[at].astype(f32)
        sig = 0.5 * jnp.tanh(0.5 * z) + 0.5
        act = z * sig
        grouped = y * act
        inv = lax.rsqrt(jnp.sum(grouped * grouped, axis=1, keepdims=True) * (1.0 / channels) + EPS)
        normed = grouped * inv
        mixed[at] = (normed * gain_row).astype(bf16)
        g_norm = (frozen[at].astype(f32) + g_mixed[at]) * gain_row
        mean = jnp.sum(g_norm * normed, axis=1, keepdims=True) * (1.0 / channels)
        g_grouped = inv * (g_norm - normed * mean)
        gate_grad[at] = (g_grouped * y * (sig + act * (1.0 - sig))).astype(bf16)
        exact = g_grouped * act * fall
        g = exact.astype(bf16)
        gye[at] = g
        gye_low[at] = (exact - g.astype(f32)).astype(bf16)
        high, low = split2(g.astype(f32) * within)
        product[0, at] = high
        product[1, at] = low
        return carry

    lax.fori_loop(0, length // ROWS, tile, 0, unroll=length // ROWS)
    state_grad[...] = dot(cstart[...], gye[...], 0, 0) * rows[1:2]
    u_here = dot(down[...], mixed[...], 1, 1)
    u_part[...] = u_here if first == 0 else u_here + u_before[...]
    down_part = dot(gu, mixed[...], 1, 0)
    split_rows(odd, down_part, keep, send)
    ones = places.astype(bf16)
    y_dot[...] = dot(ones, product[0], 1, 1) + dot(ones, product[1], 1, 1)


def pair_kernel(b, c, ids_row, ids_col, xw, gye, gye_low, scaled_in, c_grad, z_loc, b_loc):
    length = b.shape[0]
    half = length // 2
    scaled = scaled_in[...]
    for i in range(2):
        here = pl.ds(i * half, half)
        carried = dot(gye[here], scaled, 1, 1)
        total = jnp.where(ids_col[here, 0:1] == 0, carried, 0.0)
        for j in range(i + 1):
            there = pl.ds(j * half, half)
            same = ids_col[here, 0:1] == ids_row[0:1, there]
            if i == j:
                r = lax.broadcasted_iota(jnp.int32, (half, half), 0)
                s = lax.broadcasted_iota(jnp.int32, (half, half), 1)
                same = same & (r >= s)
            cross = dot(gye[here], xw[there], 1, 1) + dot(gye_low[here], xw[there], 1, 1)
            pair = jnp.where(same, cross, 0.0).astype(bf16)
            total += dot(pair, b[there], 1, 0)
        c_grad[here] = total.astype(bf16)
    for j in range(2):
        there = pl.ds(j * half, half)
        z_total = None
        for i in range(j, 2):
            here = pl.ds(i * half, half)
            same = ids_col[there, 0:1] == ids_row[0:1, here]
            if i == j:
                s = lax.broadcasted_iota(jnp.int32, (half, half), 0)
                r = lax.broadcasted_iota(jnp.int32, (half, half), 1)
                same = same & (r >= s)
            m = jnp.where(same, dot(b[there], c[here], 1, 1), 0.0).astype(bf16)
            cross = dot(xw[there], gye[here], 1, 1) + dot(xw[there], gye_low[here], 1, 1)
            pair = jnp.where(same, cross, 0.0).astype(bf16)
            z_term = dot(m, gye[here], 1, 0)
            b_term = dot(pair, c[here], 1, 0)
            z_total = z_term if z_total is None else z_total + z_term
            b_total = b_term if i == j else b_total + b_term
        z_loc[there] = z_total
        b_loc[there] = b_total


def input_kernel(
    z_loc, b_loc, bend, ids_col, ids_row, xw, gye, near, far, mid, grad_dev, scaled_in, rows, small, skips,
    rates, y_dot, passing,
    x_grad, b_grad, step_grad, passed,
    inner, weights, rises, product,
    first,
):
    length, channels = xw.shape
    heads = channels // HEAD
    skip = head_column(skips[...], heads, first)
    rate = head_column(rates[...], heads, first)
    places = head_places(heads, channels)
    dt = small[0:heads]
    rise = small[2 * heads : 3 * heads]
    raw = small[3 * heads :]
    incoming = gather_incoming(near, far, mid)
    passed[...] = passing[...]
    scaled = (incoming * rows[1:2]).astype(bf16)
    inner[...] = z_loc[...] + dot(bend[...], scaled, 1, 0)
    weights[...] = spread(dt * rise, places)
    rises[...] = spread(skip * rise, places)

    def tile(i, carry):
        at = pl.ds(pl.multiple_of(i * ROWS, ROWS), ROWS)
        z = inner[at]
        x_grad[at] = (weights[at] * z + rises[at] * gye[at].astype(f32)).astype(bf16)
        high, low = split2(xw[at].astype(f32) * z)
        product[0, at] = high
        product[1, at] = low
        return carry

    lax.fori_loop(0, length // ROWS, tile, 0, unroll=length // ROWS)
    carried = dot(xw[...], scaled, 1, 1)
    to_end = ids_col[:, 0:1] == ids_row[0:1, length - 1 :]
    b_grad[...] = (b_loc[...] + jnp.where(to_end, carried, 0.0)).astype(bf16)
    ones = places.astype(bf16)
    x_dot = dot(ones, product[0], 1, 1) + dot(ones, product[1], 1, 1)
    crossing = jnp.sum(
        (rows[0:1] * incoming + grad_dev[...]) * scaled_in[...].astype(f32), axis=0, keepdims=True
    ) / rows[1:2]
    constant = jnp.sum(jnp.where(places, crossing, 0.0), axis=1, keepdims=True)
    g_log = running_sum(x_dot - y_dot[...], True) + constant
    g_dt = x_dot / dt - rate * g_log
    step_grad[...] = g_dt / (1.0 + jnp.exp(-raw))


def adapter_kernel(u_here, u_there, up, lo, out, up_part):
    u = (SCALE * (u_here[...] + u_there[...])).astype(bf16)
    out[...] = dot(u, up[...], 0, 0).astype(bf16)
    up_part[...] = dot(u, lo[...], 1, 0)


def output_kernel(u, up, out):
    out[...] = dot(u[...], up[...], 0, 0).astype(bf16)


def halves_kernel(
    odd, u_here, u_there, lo, keep_down, send_down, decay_in, u_out, keep, send, decay
):
    u = (SCALE * (u_here[...] + u_there[...])).astype(bf16)
    u_out[...] = u
    rows = keep_down.shape[0]
    split_rows(odd, dot(u, lo[...], 1, 0), keep.at[:rows], send.at[:rows])
    keep[rows:] = keep_down[...]
    send[rows:] = send_down[...]
    decay[...] = decay_in[...]


def join_kernel(odd, keep, got, up_out, down_out):
    is_odd = odd[0:1, 0:1] == 1
    rows = keep.shape[0] // 2
    for at, out in ((pl.ds(0, rows), up_out), (pl.ds(rows, rows), down_out)):
        out[:rows] = jnp.where(is_odd, got[at], keep[at])
        out[rows:] = jnp.where(is_odd, keep[at], got[at])


def rank_kernel(up, lo, odd, part, marks):
    marks[...] = odd[...]
    part[...] = dot(up[...], lo[...], 1, 1)


def call(kernel, ins, outs, scratch=(), cost=1.0, name=None):
    in_specs, operands = [], []
    for array, block, index, *pinned in ins:
        if pinned:
            array = pltpu.with_memory_space_constraint(array, pltpu.HBM)
        if block in ("scalar", "far"):
            space = pltpu.SMEM if block == "scalar" else pltpu.HBM
            in_specs.append(pl.BlockSpec(memory_space=space))
            operands.append(array)
            continue
        if block is None:
            block, index = array.shape, (0,) * array.ndim
        in_specs.append(pl.BlockSpec(block, functools.partial(lambda at, i: at, index)))
        operands.append(array)
    out_specs, out_shapes, aliases = [], [], {}
    for at, (shape, dtype, block, index, held, *pinned) in enumerate(outs):
        if block is None:
            block, index = shape, (0,) * len(shape)
        out_specs.append(pl.BlockSpec(block, functools.partial(lambda at, i: at, index)))
        out_shapes.append((pltpu.HBM if pinned else jax.ShapeDtypeStruct)(shape, dtype))
        if held is not None:
            aliases[len(operands)] = at
            operands.append(held)
            in_specs.append(pl.BlockSpec(memory_space=pl.ANY))
    n_real = len(ins)
    n_held = len(operands) - n_real

    def body(*refs):
        kernel(*refs[:n_real], *refs[n_real + n_held :])

    return pl.pallas_call(
        body,
        grid=(1,),
        in_specs=in_specs,
        out_specs=out_specs,
        out_shape=out_shapes,
        scratch_shapes=list(scratch),
        input_output_aliases=aliases,
        compiler_params=pltpu.CompilerParams(vmem_limit_bytes=VMEM),
        cost_estimate=pl.CostEstimate(
            flops=0, bytes_accessed=int(cost * COST), transcendentals=0
        ),
        name=name,
    )(*operands)


def after(value, *others):
    return lax.optimization_barrier((value, *others))[0]


def hop(part, axis, *pairs):
    return lax.ppermute(part, axis, list(pairs))


def chain(state, decay, axis, reverse):
    count = lax.axis_size(axis)
    incoming = jnp.zeros_like(state)
    out = state
    for at in range(count - 1):
        got = hop(out, axis, (count - 1 - at, count - 2 - at) if reverse else (at, at + 1))
        incoming = incoming + got
        out = state + decay * got
    return incoming, jnp.zeros_like(state), jnp.zeros_like(state)


def exchange_pair(part, axes, *before):
    other = None
    for axis in axes:
        count = lax.axis_size(axis)
        span = 1
        while span < count:
            part = part if other is None else after(part, *before) + other
            other = lax.ppermute(part, axis, [(i, i ^ span) for i in range(count)])
            span *= 2
    return part, other


def exchange_sum(part, axes):
    here, there = exchange_pair(part, axes)
    return here + there


def per_device(
    mixer_input_channels,
    gate_channels,
    input_group_maps,
    output_group_maps,
    step_size_input,
    resets,
    head_decay_rate,
    step_size_bias,
    skip,
    gated_norm_gain,
    adapter_down_map,
    adapter_up_map,
    frozen_mixed_gradient,
    layer_output_gradient,
):
    length, channels = mixer_input_channels.shape
    groups = input_group_maps.shape[1] // STATE
    heads = step_size_input.shape[0] // groups
    width = channels // groups
    rank = adapter_up_map.shape[0]
    resets = resets.reshape(1, length)
    rates = head_decay_rate.reshape(1, -1)
    biases = step_size_bias.reshape(1, -1)
    skips = skip.reshape(1, -1)
    down_map = adapter_down_map.T
    gains = gated_norm_gain.reshape(1, -1)

    def cols(array, g):
        return (array, (array.shape[0], array.shape[1] // groups), (0, g))

    def head_rows(array, g):
        return (array, (heads, array.shape[1]), (g, 0))

    def whole(array):
        return (array, None, None)

    def fresh(shape, dtype):
        return (shape, dtype, None, None, None)

    def far(array):
        return (array, "far", None, True)

    def slow(item):
        return (*item, True)

    everything = range(groups)
    short = lax.axis_size("ctx") == 4

    def state_call(g, rates):
        return call(
            functools.partial(state_kernel, first=g * heads),
            [
                slow(cols(mixer_input_channels, g)),
                slow(cols(input_group_maps, g)),
                slow(cols(output_group_maps, g)),
                slow(head_rows(step_size_input, g)),
                slow(whole(resets)),
                slow(whole(rates)),
                slow(whole(biases)),
            ],
            [
                fresh((length, width), bf16),
                fresh((STATE, width), f32),
                slow(fresh((length, STATE), bf16)),
                fresh((length, STATE), bf16),
                fresh((4 * heads, length), f32),
                fresh((8, width), f32),
                fresh((8, length), f32),
                fresh((length, 8), f32),
            ],
            cost=1.5,
            name="state",
        )

    def score_call(g, *before):
        xw, _, _, _, _, _, ids_row, ids_col = states[g]
        ids_row = after(ids_row, *before) if before else ids_row
        return call(
            score_kernel,
            [
                cols(input_group_maps, g),
                cols(output_group_maps, g),
                whole(ids_row),
                whole(ids_col),
                whole(xw),
            ],
            [fresh((length, width), f32)],
            cost=1.0,
            name="score",
        )[0]

    paired = short and groups == 2
    odd = jnp.full((8, 128), lax.axis_index("ctx") % 2 if paired else 0, jnp.int32)

    def rank_call(*before):
        return call(
            rank_kernel,
            [
                whole(after(adapter_up_map, *before) if before else adapter_up_map),
                whole(layer_output_gradient),
                whole(odd),
            ],
            [fresh((rank, length), f32), fresh((8, 128), jnp.int32)],
            cost=1.0,
            name="rank",
        )

    states, y_locs = [state_call(0, rates)], []
    gu_part, marks = rank_call(states[0][5])
    for g in range(1, groups):
        states.append(state_call(g, after(rates, gu_part)))

    parts = [states[g][1] for g in everything]
    decays = [states[g][5][0:1] for g in everything]
    entering = []
    if short:
        first = [hop(parts[g], "ctx", (0, 1)) for g in everything]
        gu = exchange_pair(gu_part, ("fsdp", "head"), states[-1][5])
        y_locs.append(score_call(0, gu[0]))
        joined = [after(decays[g], y_locs[0]) * first[g] + parts[g] for g in everything]
        second = [hop(joined[g], "ctx", (1, 2)) for g in everything]
        joined = decays[0] * second[0] + parts[0]
        third = [hop(joined, "ctx", (2, 3))]
        for g in range(1, groups):
            y_locs.append(score_call(g, joined))
            joined = after(decays[g], y_locs[-1], gu[1]) * second[g] + parts[g]
            third.append(hop(joined, "ctx", (2, 3)))
        entering = list(zip(first, second, third))
    else:
        y_locs = [score_call(g) for g in everything]
        gu = exchange_pair(gu_part, ("fsdp", "head"))
        entering = [chain(parts[g], decays[g], "ctx", False) for g in everything]
    mixed = gate_grad = keep_down = send_down = u_part = c_grad = None
    normed, pairs = [], []

    def pair_call(g, held, *others):
        xw, state, bend, cstart, small, rows, ids_row, ids_col = states[g]
        return call(
            pair_kernel,
            [
                cols(input_group_maps, g),
                cols(output_group_maps, g),
                whole(after(ids_row, *others) if others else ids_row),
                whole(ids_col),
                whole(xw),
                whole(normed[g][0]),
                slow(whole(normed[g][5])),
                whole(normed[g][1]),
            ],
            [
                ((length, groups * STATE), bf16, (length, STATE), (0, g), held),
                fresh((length, width), f32),
                fresh((length, STATE), f32),
            ],
            cost=2.0,
            name="pair",
        )

    for g in everything:
        xw, state, bend, cstart, small, rows, ids_row, ids_col = states[g]
        results = call(
            functools.partial(norm_kernel, first=g * heads),
            [
                whole(marks),
                whole(y_locs[g]),
                whole(cstart),
                *map(whole, entering[g]),
                whole(small),
                whole(rows),
                cols(mixer_input_channels, g),
                cols(gate_channels, g),
                whole(skips),
                cols(gains, g),
                cols(frozen_mixed_gradient, g),
                *map(whole, gu),
                cols(down_map, g),
            ]
            + ([] if g == 0 else [whole(u_part)]),
            [
                ((length, channels), bf16, (length, width), (0, g), mixed),
                ((length, channels), bf16, (length, width), (0, g), gate_grad),
                slow(((rank // 2, channels), f32, (rank // 2, width), (0, g), keep_down)),
                slow(((rank // 2, channels), f32, (rank // 2, width), (0, g), send_down)),
                (slow if g < groups - 1 else tuple)(fresh((length, width), bf16)),
                slow(fresh((STATE, width), bf16)),
                fresh((STATE, width), f32),
                fresh((rank, length), f32),
                slow(fresh((heads, length), f32)),
                (slow if g == groups - 1 else tuple)(fresh((1, width), f32)),
                slow(fresh((length, width), bf16)),
            ],
            [
                pltpu.VMEM((length, width), f32),
                pltpu.VMEM((length, width), f32),
                pltpu.VMEM((length, width), f32),
                pltpu.VMEM((2, length, width), bf16),
            ],
            cost=4.0,
            name="norm",
        )
        mixed, gate_grad, keep_down, send_down, gye, scaled, state_grad, u_part, y_dot, decay, gye_low = results
        normed.append((gye, scaled, state_grad, y_dot, decay, gye_low))
    def input_call(g, leaving, held, passing, *before):
        xw, state, bend, cstart, small, rows, ids_row, ids_col = states[g]
        x_grad, b_grad, step_grad = held
        return call(
            functools.partial(input_kernel, first=g * heads),
            [
                whole(pairs[g][0]),
                whole(pairs[g][1]),
                whole(bend),
                whole(ids_col),
                whole(ids_row),
                whole(xw),
                whole(normed[g][0]),
                *map(whole, leaving),
                whole(normed[g][2]),
                whole(normed[g][1]),
                whole(rows),
                whole(small),
                whole(skips),
                whole(after(rates, *before) if before else rates),
                slow(whole(normed[g][3])),
                whole(passing),
            ],
            [
                ((length, channels), bf16, (length, width), (0, g), x_grad),
                ((length, groups * STATE), bf16, (length, STATE), (0, g), b_grad),
                ((groups * heads, length), f32, (heads, length), (g, 0), step_grad),
                fresh(passing.shape, f32),
            ],
            [
                pltpu.VMEM((length, width), f32),
                pltpu.VMEM((length, width), f32),
                pltpu.VMEM((length, width), f32),
                pltpu.VMEM((2, length, width), bf16),
            ],
            cost=2.5,
            name="input",
        )

    state_grads = [normed[g][2] for g in everything]
    decays = [normed[g][4] for g in everything]
    held = (None, None, None)
    if paired:
        neighbours = [(0, 1), (1, 0), (2, 3), (3, 2)]
        across = [(0, 2), (2, 0), (1, 3), (3, 1)]
        last = [hop(state_grads[g], "ctx", (3, 2)) for g in everything]
        sent = after(decays[0], u_part) * last[0] + state_grads[0]
        then = [hop(sent, "ctx", (2, 1))]
        u = exchange_pair(u_part, ("fsdp", "head"), sent)
        half = fresh((rank, channels), f32)
        u, keep, send, decay = call(
            halves_kernel,
            [
                whole(odd),
                *map(whole, u),
                whole(layer_output_gradient),
                slow(whole(keep_down)),
                slow(whole(send_down)),
                slow(whole(decays[1])),
            ],
            [fresh((rank, length), bf16), half, half, fresh((1, width), f32)],
            cost=1.5,
            name="halves",
        )
        sent = decay * last[1] + state_grads[1]
        then.append(hop(sent, "ctx", (2, 1)))
        got = hop(send, "ctx", *neighbours)
        sent = after(decays[0], sent) * then[0] + state_grads[0]
        ahead = [hop(sent, "ctx", (1, 0))]
        c_grad, *pair = pair_call(0, c_grad, sent)
        pairs.append(pair)
        sent = after(decay, pair[1]) * then[1] + state_grads[1]
        ahead.append(hop(sent, "ctx", (1, 0)))
        keep = after(keep, sent) + got
        got = hop(keep, "ctx", *across)
        c_grad, *pair = pair_call(1, c_grad, keep)
        pairs.append(pair)
        *held, _ = input_call(0, (last[0], then[0], ahead[0]), held, decay, pair[1])
        (adapter_output,) = call(
            output_kernel,
            [whole(after(u, pair[1])), whole(adapter_up_map)],
            [fresh((length, channels), bf16)],
            name="output",
        )
        keep = after(keep, held[2]) + got
        got = hop(keep, "ctx", *neighbours)
        *held, _ = input_call(1, (last[1], then[1], ahead[1]), held, decay)
        up_sum, down_sum = call(
            join_kernel,
            [whole(odd), whole(after(keep, held[2])), whole(got)],
            [fresh((rank, channels), f32), fresh((rank, channels), f32)],
            name="join",
        )
    else:
        u = exchange_pair(u_part, ("fsdp", "head"))
        adapter_output, up_part = call(
            adapter_kernel,
            [*map(whole, u), whole(adapter_up_map), whole(layer_output_gradient)],
            [fresh((length, channels), bf16), fresh((rank, channels), f32)],
            cost=1.5,
            name="adapter",
        )
        for g in everything:
            c_grad, *pair = pair_call(g, c_grad)
            pairs.append(pair)
            leaving = chain(state_grads[g], decays[g], "ctx", True)
            *held, _ = input_call(g, leaving, held, decays[g])
        up_sum = exchange_sum(up_part, ("ctx",))
        down_sum = exchange_sum(jnp.concatenate([keep_down, send_down], axis=0), ("ctx",))
    x_grad, b_grad, step_grad = held
    return (
        mixed,
        adapter_output,
        x_grad,
        gate_grad,
        b_grad,
        c_grad,
        step_grad,
        down_sum.T,
        up_sum,
    )


def solution(mesh):
    rows_cols = P(("parts", "ctx"), ("head", "fsdp"))
    heads = P(("head", "fsdp"))
    in_specs = (
        rows_cols,
        rows_cols,
        rows_cols,
        rows_cols,
        P(("head", "fsdp"), ("parts", "ctx")),
        P(("parts", "ctx")),
        heads,
        heads,
        heads,
        heads,
        P(("head", "fsdp"), None),
        P(None, ("head", "fsdp")),
        rows_cols,
        rows_cols,
    )
    out_specs = (
        rows_cols,
        rows_cols,
        rows_cols,
        rows_cols,
        rows_cols,
        rows_cols,
        P(("head", "fsdp"), ("parts", "ctx")),
        P(("parts", "head", "fsdp"), None),
        P("parts", ("head", "fsdp")),
    )
    return jax.shard_map(
        per_device, mesh=mesh, in_specs=in_specs, out_specs=out_specs, check_vma=False
    )
```
